256 devices in a mesh: head: 8 (over z_hi, core), inner: 4 (over y), outer: 8 (over z_lo, x).
Axes of the slice: x: 4, y: 4, z: 8 (z_hi: 4, z_lo: 2; z = z_hi * 2 + z_lo), core: 2. Of those that a mesh axis runs over, the one named last changes fastest.
Arguments:
- queries: bfloat16 [7680, 4096], P(('inner', 'outer', 'head')), may hold values from -8 to 8
- keys: bfloat16 [7680, 1024], P(('inner', 'outer', 'head')), may hold values from -8 to 8
- values: bfloat16 [7680, 1024], P(('inner', 'outer', 'head')), may hold values from -6 to 6
- grad_out: bfloat16 [7680, 4096], P(('inner', 'outer', 'head')), may hold values from -6 to 6
- doc_lengths: int32 [16], replicated, may hold values from 1 to 768, 7680 in all
- positions: int32 [7680], replicated, may hold values from 0 to 7679, as said below
Outputs:
- attention: bfloat16 [7680, 4096], P(('inner', 'outer', 'head'))
- grad_queries: bfloat16 [7680, 4096], P(('inner', 'outer', 'head'))
- grad_keys: bfloat16 [7680, 1024], P(('inner', 'outer', 'head'))
- grad_values: bfloat16 [7680, 1024], P(('inner', 'outer', 'head'))
The draws below stay inside these ranges and needn't reach their ends.
Inputs may be any that keep to these rules, and one draw needn't show every extreme that they name: Each aligned run of 128 rows holds 128 consecutive positions in increasing order; every position appears once. `doc_lengths`: the lengths sum to 7680; the largest is exactly 768.
All inputs are finite; a program needn't handle non-finite values.
Results may differ from the reference program's by a relative error of at most 0.03.
Values may be sent and summed in bfloat16 or wider, within the bound.
No kernel may reach another device: no remote copies, remote signals or barrier semaphores. Data moves between devices by JAX's collectives and lax.ppermute only.
A program may use at most 128 MiB of HBM per device.

```python
import math
import jax
import jax.numpy as jnp
import numpy as np
from jax import lax

HD = 128
GROUP = 4
HEADS_KV = 8
HQ = 32
SEQ = 7680
NDOC = 16
DOC_MOST = 768
RUN = 128


def draw_queries(key, part):
    key = jax.random.fold_in(key, 11)
    second = jax.random.fold_in(key, 1)
    columns = GROUP * HEADS_KV * HD
    drawn = jax.random.truncated_normal(second, -6.0, 6.0, (SEQ, columns))
    return drawn.astype(jnp.float32).astype(jnp.bfloat16)


def draw_keys(key, part):
    key = jax.random.fold_in(key, 23)
    second = jax.random.fold_in(key, 1)
    columns = HEADS_KV * HD
    drawn = jax.random.truncated_normal(second, -6.0, 6.0, (SEQ, columns))
    return drawn.astype(jnp.float32).astype(jnp.bfloat16)


def draw_positions(key, part):
    key = jax.random.fold_in(key, 37)
    placed = jax.random.permutation(key, jnp.arange(SEQ // RUN, dtype=jnp.int32))
    rows = jnp.arange(SEQ, dtype=jnp.int32)
    return (placed[rows // RUN] * RUN + rows % RUN).astype(jnp.int32)


def shard_levels(rng, extent, cuts, low, high):
    def one(axis_at, parts):
        steps = jax.random.uniform(jax.random.fold_in(jax.random.fold_in(rng, 6), axis_at), (parts,), jnp.float32, low / len(cuts), high / len(cuts))
        return jnp.repeat(jnp.exp(steps), extent[axis_at] // parts).reshape((-1,) + (1,) * (len(extent) - axis_at - 1))

    loudness = one(*cuts[0])
    for cut in cuts[1:]:
        loudness = loudness * one(*cut)
    return loudness


def profile(amount, total, limit, lean):
    weights = [(1 << 20) // math.isqrt(standing ** lean) + 1 for standing in range(2, amount + 1)]
    spare, given = total - limit - (amount - 1), [1] * (amount - 1)
    while spare > 0:
        free = [i for i in range(amount - 1) if given[i] < limit]
        whole, left = sum([weights[i] for i in free]), spare
        for i in free:
            more = min(limit - given[i], max(1, left * weights[i] // whole), spare)
            given[i] = given[i] + more
            spare = spare - more
    return np.array([limit] + given)


def ragged(key, amount, total, most, slope):
    if amount == 2:
        one = jax.random.randint(key, (), max(1, total - most), min(most, total - 1) + 1)
        return jnp.stack([one, total - one])
    tallies = jnp.asarray(profile(amount, total, most, slope), jnp.int32)
    couples = (amount - 1) // 2
    donor, taker = tallies[1:1 + 2 * couples:2], tallies[2:2 + 2 * couples:2]
    room = jnp.minimum(donor - 1, most - taker)
    moved = jax.random.randint(jax.random.fold_in(key, 1), (couples,), 0, 1 << 20) % (room + 1)
    tallies = tallies.at[1:1 + 2 * couples:2].set(donor - moved).at[2:2 + 2 * couples:2].set(taker + moved)
    return tallies[jax.random.permutation(jax.random.fold_in(key, 2), amount)]


def normal_values(key, dims, spread, bound, cuts=(), kind=jnp.bfloat16):
    array = jax.random.normal(key, dims, jnp.float32) * spread
    if len(cuts) > 0:
        array = shard_levels(key, dims, cuts, -0.22, 0.18) * array
    return jnp.clip(array, min=-bound, max=bound).astype(kind)


def setup_inputs(seed: int = 0) -> dict:
    streams_of = jax.random.split(jax.random.key(seed), 7)
    return {
        "queries": draw_queries(jax.random.fold_in(streams_of[6], 71), 0),
        "keys": draw_keys(jax.random.fold_in(streams_of[6], 71), 0),
        "values": normal_values(streams_of[2], (SEQ, HEADS_KV * HD), 1.0, 6.0, ((0, 256),)),
        "grad_out": normal_values(streams_of[3], (SEQ, HQ * HD), 1.0, 6.0, ((0, 256),)),
        "doc_lengths": ragged(streams_of[4], NDOC, SEQ, DOC_MOST, 1).astype(jnp.int32),
        "positions": draw_positions(jax.random.fold_in(streams_of[6], 71), 0),
    }


negative = -1e30


def document_of(where_pos, ends):
    return jnp.sum((ends[None, :] <= where_pos[:, None]).astype(jnp.int32), axis=1)


def reference(queries, keys, values, grad_out, doc_lengths, positions):
    total = positions.shape[0]
    ends = jnp.cumsum(doc_lengths).astype(jnp.int32)
    order = jnp.arange(total, dtype=jnp.int32)
    inverse = jnp.zeros((total,), jnp.int32).at[positions].set(order)
    block = math.gcd(total, 512)
    reach = DOC_MOST
    span = reach + block
    scale = HD ** -0.5
    query_doc = document_of(order, ends)
    key_pos = jnp.concatenate([jnp.full((reach,), -1, jnp.int32), order])
    key_doc = document_of(key_pos, ends)
    padding = jnp.zeros((reach, HEADS_KV * HD), jnp.bfloat16)
    key_rows = jnp.concatenate([padding, keys[inverse]])
    value_rows = jnp.concatenate([padding, values[inverse]])
    query_rows = queries[inverse]
    grad_rows = grad_out[inverse]

    def one_head(index):
        query_head = lax.dynamic_slice_in_dim(query_rows, index * GROUP * HD, GROUP * HD, 1).reshape(total, GROUP, HD)
        grad_head = lax.dynamic_slice_in_dim(grad_rows, index * GROUP * HD, GROUP * HD, 1).reshape(total, GROUP, HD)
        key_head = lax.dynamic_slice_in_dim(key_rows, index * HD, HD, 1)
        value_head = lax.dynamic_slice_in_dim(value_rows, index * HD, HD, 1)

        def visit(carry, number):
            grad_k_acc, grad_v_acc = carry
            start = number * block
            query_b = lax.dynamic_slice_in_dim(query_head, start, block, 0).astype(jnp.float32)
            grad_b = lax.dynamic_slice_in_dim(grad_head, start, block, 0).astype(jnp.float32)
            key_b = lax.dynamic_slice_in_dim(key_head, start, span, 0).astype(jnp.float32)
            value_b = lax.dynamic_slice_in_dim(value_head, start, span, 0).astype(jnp.float32)
            kpos = lax.dynamic_slice_in_dim(key_pos, start, span)
            kdoc = lax.dynamic_slice_in_dim(key_doc, start, span)
            qpos = start + jnp.arange(block, dtype=jnp.int32)
            qdoc = lax.dynamic_slice_in_dim(query_doc, start, block)
            mask = (kdoc[None, :] == qdoc[:, None]) & (kpos[None, :] <= qpos[:, None]) & (kpos[None, :] >= 0)
            mask3 = mask[:, None, :]
            scores = jnp.einsum("rgd,kd->rgk", query_b, key_b) * scale
            scores = jnp.where(mask3, scores, negative)
            top = jnp.max(scores, axis=2)
            weights = jnp.where(mask3, jnp.exp(scores - top[..., None]), 0.0)
            summed = jnp.sum(weights, axis=2)
            output = jnp.einsum("rgk,kd->rgd", weights.astype(jnp.bfloat16).astype(jnp.float32), value_b)
            output = (output / summed[..., None]).astype(jnp.bfloat16)
            log_total = top + jnp.log(summed)
            delta = jnp.sum(grad_b * output.astype(jnp.float32), axis=2)
            prob = jnp.where(mask3, jnp.exp(scores - log_total[..., None]), 0.0)
            dprob = jnp.einsum("rgd,kd->rgk", grad_b, value_b)
            dscore = (prob * (dprob - delta[..., None])).astype(jnp.bfloat16).astype(jnp.float32)
            prob_low = prob.astype(jnp.bfloat16).astype(jnp.float32)
            grad_q = (jnp.einsum("rgk,kd->rgd", dscore, key_b) * scale).astype(jnp.bfloat16)
            key_term = jnp.einsum("rgk,rgd->kd", dscore, query_b) * scale
            value_term = jnp.einsum("rgk,rgd->kd", prob_low, grad_b)
            grad_k_acc = lax.dynamic_update_slice_in_dim(grad_k_acc, lax.dynamic_slice_in_dim(grad_k_acc, start, span, 0) + key_term, start, 0)
            grad_v_acc = lax.dynamic_update_slice_in_dim(grad_v_acc, lax.dynamic_slice_in_dim(grad_v_acc, start, span, 0) + value_term, start, 0)
            return (grad_k_acc, grad_v_acc), (output, grad_q)

        empty = jnp.zeros((reach + total, HD), jnp.float32)
        (grad_k_acc, grad_v_acc), (outputs, grads) = lax.scan(visit, (empty, empty), jnp.arange(total // block, dtype=jnp.int32))
        return (outputs.reshape(total, GROUP * HD), grads.reshape(total, GROUP * HD),
                grad_k_acc[reach:].astype(jnp.bfloat16), grad_v_acc[reach:].astype(jnp.bfloat16))

    outputs, grads, grad_keys, grad_values = lax.map(one_head, jnp.arange(HEADS_KV, dtype=jnp.int32))
    attention = jnp.transpose(outputs, (1, 0, 2)).reshape(total, HQ * HD)[positions]
    grad_queries = jnp.transpose(grads, (1, 0, 2)).reshape(total, HQ * HD)[positions]
    grad_keys = jnp.transpose(grad_keys, (1, 0, 2)).reshape(total, HEADS_KV * HD)[positions]
    grad_values = jnp.transpose(grad_values, (1, 0, 2)).reshape(total, HEADS_KV * HD)[positions]
    return attention, grad_queries, grad_keys, grad_values
```

```python
import jax
import jax.numpy as jnp
from jax import lax
from jax.experimental import pallas as pl
from jax.experimental.pallas import tpu as pltpu
from jax.sharding import PartitionSpec as P

HD = 128
GROUP = 4
KVH = 8
RUN = 128
BACK = 3
SPREAD = 32
BLOCK = 256
UNIT = 10
LOCAL = 30
SCALE = HD**-0.5
LOG2E = 1.4426950408889634
NEGATIVE = -1e30
ALL = ("head", "inner", "outer")
SEQ_AXES = ("inner", "outer")
LIMIT = 48 * 1024 * 1024

f32, bf16, i32 = jnp.float32, jnp.bfloat16, jnp.int32


def iota(shape, dim):
    return lax.broadcasted_iota(i32, shape, dim)


def one_hot(condition):
    return jnp.where(condition, 1.0, 0.0).astype(bf16)


def dot(a, b):
    return jnp.dot(a, b, preferred_element_type=f32)


def dot_nt(a, b):
    return lax.dot_general(a, b, (((1,), (1,)), ((), ())), preferred_element_type=f32)


def first_row():
    device = lax.axis_index("inner") * 64 + lax.axis_index("outer") * 8 + lax.axis_index("head")
    return (device * LOCAL) & (SPREAD - 1)


def seq_index():
    return lax.axis_index("inner") * 8 + lax.axis_index("outer")


def spread_row(packed, shift):
    token = packed & 31
    to = ((shift + token) & 31) * UNIT + (packed >> 5)
    return jnp.where(token < LOCAL, to, -1)


def place_spread(rows_are_units):
    size = UNIT * 32
    to = spread_row(iota((size, size), int(rows_are_units)), first_row())
    return one_hot(iota((size, size), 1 - int(rows_are_units)) == to)


def pack_kernel(q_ref, k_ref, v_ref, g_ref, out_ref, qs, ks, vs, gs, x_ref, o_ref, in_sem, out_sem):
    size = UNIT * 32
    wide, pairs = 2 * GROUP * HD, KVH // 2
    arrivals = []
    for i, (source, to) in enumerate(((k_ref, ks), (v_ref, vs))):
        arrivals.append(pltpu.make_async_copy(source, to, in_sem.at[i]))
    for pair in range(pairs):
        at = pl.ds(pair * wide, wide)
        for i, (source, to) in enumerate(((q_ref, qs), (g_ref, gs))):
            arrivals.append(
                pltpu.make_async_copy(source.at[:, at], to.at[:, at], in_sem.at[2 + 2 * pair + i])
            )
    for copy in arrivals:
        copy.start()
    x_ref[...] = jnp.zeros_like(x_ref)
    place = place_spread(True)
    departures = []
    for pair in range(pairs):
        for copy in arrivals[2 * pair + 2 : 2 * pair + 4] + (arrivals[:2] if pair == 0 else []):
            copy.wait()
        for head in (2 * pair, 2 * pair + 1):
            to = pl.ds(head * HD, HD)
            for g in range(GROUP):
                column = pl.ds((head * GROUP + g) * HD, HD)
                x_ref[pl.ds(g * 32, LOCAL), to] = qs[:, column]
                x_ref[pl.ds((GROUP + g) * 32, LOCAL), to] = gs[:, column]
            x_ref[pl.ds(8 * 32, LOCAL), to] = ks[:, to]
            x_ref[pl.ds(9 * 32, LOCAL), to] = vs[:, to]
        rows = dot(place, x_ref[:, pl.ds(pair * 2 * HD, 2 * HD)]).astype(bf16)
        o_ref[pl.ds(2 * pair * size, size), :] = rows[:, :HD]
        o_ref[pl.ds((2 * pair + 1) * size, size), :] = rows[:, HD:]
        at = pl.ds(2 * pair * size, 2 * size)
        departures.append(pltpu.make_async_copy(o_ref.at[at, :], out_ref.at[at, :], out_sem.at[pair]))
        departures[-1].start()
    for copy in departures:
        copy.wait()


def unpack_kernel(r_ref, place_ref, att_ref, gq_ref, gk_ref, gv_ref, qs, ks, vs, gs, x_ref, sem):
    size = UNIT * 32
    wide, pairs = 2 * GROUP * HD, KVH // 2
    departures = []
    for pair in range(pairs):
        for half in range(2):
            x_ref[pair, :, pl.ds(half * HD, HD)] = r_ref[pl.ds((2 * pair + half) * size, size), :]
        rows = dot(place_ref[...], x_ref[pair]).astype(bf16)
        for half in range(2):
            head = 2 * pair + half
            part = rows[:, half * HD : (half + 1) * HD]
            to = pl.ds(head * HD, HD)
            for g in range(GROUP):
                column = pl.ds((head * GROUP + g) * HD, HD)
                qs[:, column] = part[g * 32 : g * 32 + LOCAL]
                gs[:, column] = part[(GROUP + g) * 32 : (GROUP + g) * 32 + LOCAL]
            ks[:, to] = part[8 * 32 : 8 * 32 + LOCAL]
            vs[:, to] = part[9 * 32 : 9 * 32 + LOCAL]
        at = pl.ds(pair * wide, wide)
        for source, to in ((qs, att_ref), (gs, gq_ref)):
            departures.append(
                pltpu.make_async_copy(source.at[:, at], to.at[:, at], sem.at[len(departures)])
            )
            departures[-1].start()
    for source, to in ((ks, gk_ref), (vs, gv_ref)):
        departures.append(pltpu.make_async_copy(source, to, sem.at[len(departures)]))
        departures[-1].start()
    for copy in departures:
        copy.wait()


def sender(run, slot, group):
    row = run * RUN + (slot & 3) * 32 + group
    device = (row * 34953) >> 20
    return jnp.where(run >= 0, ((device & 7) << 5) + (device >> 3), -1)


def position(row):
    return ((row >> 2) & 1) * RUN + (row & 3) * 32 + (row >> 3)


def table_kernel(
    run_row_ref, run_col_ref, lengths_ref, sort_ref, unsort_ref, unpack_ref, begin_ref
):
    group = seq_index()
    query_pos = group * BLOCK + position(iota((1, BLOCK), 1))
    begin = jnp.zeros((1, BLOCK), i32)
    end = jnp.int32(0)
    for i in range(16):
        end = end + lengths_ref[i]
        begin = jnp.where(query_pos >= end, end, begin)
    begin_ref[...] = begin
    number = iota((BLOCK, 64), 1)
    for b in range(BACK + 1):
        slot = iota((BLOCK, 1), 0)
        found = run_row_ref[...] == (slot >> 2) - 2 * b
        run = jnp.max(jnp.where(found, number, -1), axis=1, keepdims=True)
        sort_ref[pl.ds(b * BLOCK, BLOCK), :] = one_hot(
            iota((BLOCK, BLOCK), 1) == sender(run, slot, group)
        )
    slot = iota((1, BLOCK), 1)
    found = run_col_ref[...] == (slot >> 2)
    run = jnp.max(jnp.where(found, iota((64, BLOCK), 0), -1), axis=0, keepdims=True)
    unsort_ref[...] = one_hot(iota((BLOCK, BLOCK), 0) == sender(run, slot, group))
    unpack_ref[...] = place_spread(False)


def sort_kernel(r_ref, place_ref, out_ref, wide_ref, x_ref):
    wide_ref[...] = r_ref[...].astype(f32)
    for u in range(UNIT):
        x_ref[:, pl.ds(u * HD, HD)] = wide_ref[pl.ds(u, BLOCK, stride=UNIT), :].astype(bf16)
    out_ref[:, pl.ds(0, 1280)] = dot(place_ref[pl.ds(0, BLOCK), :], x_ref[...]).astype(bf16)
    for b in range(1, BACK + 1):
        out_ref[:, pl.ds(1024 + 256 * b, 256)] = dot(
            place_ref[pl.ds(b * BLOCK, BLOCK), :], x_ref[:, pl.ds(1024, 256)]
        ).astype(bf16)


def unsort_kernel(r_ref, place_ref, out_ref, wide_ref, sum_ref, x_ref):
    for b in range(BACK + 1):
        part = r_ref[b:SPREAD, :, pl.ds(1024 + 256 * b, 256)].astype(f32)
        part = part.reshape((SPREAD - b) * 8, 256)
        rows = pl.ds(0, (SPREAD - b) * 8)
        if b == 0:
            sum_ref[rows, :] = part
        else:
            sum_ref[rows, :] = sum_ref[rows, :] + part
    x_ref[:, pl.ds(0, 1024)] = r_ref[:, :, pl.ds(0, 1024)].reshape(BLOCK, 1024)
    x_ref[:, pl.ds(1024, 256)] = sum_ref[...].astype(bf16)
    for pair in range(UNIT // 2):
        rows = dot(place_ref[...], x_ref[:, pl.ds(pair * 2 * HD, 2 * HD)])
        wide_ref[pl.ds(2 * pair, BLOCK, stride=UNIT), :] = rows[:, :HD]
        wide_ref[pl.ds(2 * pair + 1, BLOCK, stride=UNIT), :] = rows[:, HD:]
    out_ref[...] = wide_ref[...].astype(bf16)


def attention_kernel(
    begin_ref, m_ref, to_ref, out_ref, bias_ref, s_ref, dp_ref, p_ref, d_ref, q_ref, g_ref, k_ref,
    v_ref, sem,
):
    base = seq_index() * BLOCK
    blocks, heads = range(BACK + 1), range(GROUP)

    def rows(b):
        return pl.ds(b * BLOCK, BLOCK)

    departures = []

    def send(first, count):
        at = pl.ds(first, count)
        departures.append(
            pltpu.make_async_copy(out_ref.at[:, at], to_ref.at[:, at], sem.at[len(departures)])
        )
        departures[-1].start()

    query_pos = base + position(iota((1, BLOCK), 1))
    begin = begin_ref[...]
    key_pos = base + position(iota((BLOCK, BLOCK), 0))
    for b in blocks:
        seen = key_pos >= begin + b * BLOCK
        if b == 0:
            seen = seen & (key_pos <= query_pos)
        bias_ref[rows(b), :] = jnp.where(seen, 0.0, NEGATIVE)
        k_ref[rows(b), :] = m_ref[:, pl.ds(1024 + 256 * b, HD)]
        v_ref[rows(b), :] = m_ref[:, pl.ds(1024 + 256 * b + HD, HD)]
    for g in heads:
        q_ref[rows(g), :] = m_ref[:, pl.ds(g * HD, HD)]
        g_ref[rows(g), :] = m_ref[:, pl.ds((GROUP + g) * HD, HD)]
    keys, values = k_ref[...], v_ref[...]
    keys_t, values_t = keys.T, values.T

    tops, inverses, deltas = [], [], []
    for g in heads:
        s = dot_nt(keys, q_ref[rows(g), :]) * (SCALE * LOG2E) + bias_ref[...]
        s_ref[:, rows(g)] = s
        tops.append(jnp.max(s, axis=0, keepdims=True))
        dp_ref[:, rows(g)] = dot_nt(values, g_ref[rows(g), :])
    for g in heads:
        weights = jnp.exp2(s_ref[:, rows(g)] - tops[g])
        s_ref[:, rows(g)] = weights
        inverse = 1.0 / jnp.sum(weights, axis=0, keepdims=True)
        output = (dot(values_t, weights.astype(bf16)) * inverse).T.astype(bf16)
        out_ref[:, pl.ds(g * HD, HD)] = output
        product = g_ref[rows(g), :].astype(f32) * output.astype(f32)
        deltas.append(jnp.sum(product.T, axis=0, keepdims=True))
        inverses.append(inverse)
    send(0, GROUP * HD)
    for g in heads:
        prob = s_ref[:, rows(g)] * inverses[g]
        p_ref[:, rows(g)] = prob.astype(bf16)
        dscore = (prob * (dp_ref[:, rows(g)] - deltas[g])).astype(bf16)
        d_ref[:, rows(g)] = dscore
        out_ref[:, pl.ds((GROUP + g) * HD, HD)] = (dot(keys_t, dscore) * SCALE).T.astype(bf16)
    send(GROUP * HD, GROUP * HD)
    for b in blocks:
        at = 2 * GROUP * HD + 2 * HD * b
        out_ref[:, pl.ds(at, HD)] = (dot(d_ref[rows(b), :], q_ref[...]) * SCALE).astype(bf16)
        out_ref[:, pl.ds(at + HD, HD)] = dot(p_ref[rows(b), :], g_ref[...]).astype(bf16)
        send(at, 2 * HD)
    for copy in departures:
        copy.wait()


VMEM = pl.BlockSpec(memory_space=pltpu.VMEM)
ANY = pl.BlockSpec(memory_space=pl.ANY)


def call(kernel, outs, scratch, *args, place_in=VMEM, place_out=VMEM, limit=LIMIT):
    return pl.pallas_call(
        kernel,
        out_shape=[jax.ShapeDtypeStruct(o, bf16) for o in outs],
        in_specs=[place_in] * len(args),
        out_specs=[place_out] * len(outs),
        scratch_shapes=scratch,
        compiler_params=pltpu.CompilerParams(vmem_limit_bytes=limit),
    )(*args)


def exchange(x, axes):
    return lax.all_to_all(x, axes, split_axis=0, concat_axis=0, tiled=True)


def per_device(queries, keys, values, grad_out, doc_lengths, positions):
    units, size = 256 * UNIT, UNIT * 32
    wide, narrow = (LOCAL, KVH * GROUP * HD), (LOCAL, KVH * HD)
    local = [pltpu.VMEM(s, bf16) for s in (wide, narrow, narrow, wide)]
    runs = jnp.pad(positions[::RUN] // RUN, (0, 4), constant_values=-1000)
    table = pl.pallas_call(
        table_kernel,
        out_shape=[
            jax.ShapeDtypeStruct(((BACK + 1) * BLOCK, BLOCK), bf16),
            jax.ShapeDtypeStruct((BLOCK, BLOCK), bf16),
            jax.ShapeDtypeStruct((size, size), bf16),
            jax.ShapeDtypeStruct((1, BLOCK), i32),
        ],
        in_specs=[VMEM, VMEM, pl.BlockSpec(memory_space=pltpu.SMEM)],
        out_specs=[VMEM] * 4,
        compiler_params=pltpu.CompilerParams(vmem_limit_bytes=LIMIT),
        cost_estimate=pl.CostEstimate(flops=1 << 24, bytes_accessed=1 << 18, transcendentals=0),
    )
    place_sort, place_unsort, place_unpack, begin = table(
        runs.reshape(1, 64), runs.reshape(64, 1), doc_lengths
    )
    (packed,) = call(
        pack_kernel,
        [(units, HD)],
        local
        + [
            pltpu.VMEM((size, KVH * HD), bf16),
            pltpu.VMEM((units, HD), bf16),
            pltpu.SemaphoreType.DMA((10,)),
            pltpu.SemaphoreType.DMA((4,)),
        ],
        queries,
        keys,
        values,
        grad_out,
        place_in=ANY,
        limit=None,
        place_out=ANY,
    )
    spread = exchange(packed.reshape(256, UNIT // 2, 2, HD), ALL).reshape(units, HD)
    (ordered,) = call(
        sort_kernel,
        [(BLOCK, 2048)],
        [pltpu.VMEM((units, HD), f32), pltpu.VMEM((BLOCK, 1280), bf16)],
        spread,
        place_sort,
    )
    block = exchange(ordered.reshape(SPREAD, 8, 2048), SEQ_AXES).reshape(BLOCK, 2048)
    square = (GROUP * BLOCK, (BACK + 1) * BLOCK)
    (done,) = call(
        attention_kernel,
        [(BLOCK, 2048)],
        [
            pltpu.VMEM((BLOCK, 2048), bf16),
            pltpu.VMEM((square[1], BLOCK), f32),
            pltpu.VMEM(square, f32),
            pltpu.VMEM(square, f32),
            pltpu.VMEM(square, bf16),
            pltpu.VMEM(square, bf16),
        ]
        + [pltpu.VMEM((square[0], HD), bf16)] * 4
        + [pltpu.SemaphoreType.DMA((6,))],
        begin,
        block,
        place_out=ANY,
    )
    back = exchange(done.reshape(SPREAD, 8, 2048), SEQ_AXES)
    (unsorted,) = call(
        unsort_kernel,
        [(units, HD)],
        [
            pltpu.VMEM((units, HD), f32),
            pltpu.VMEM((BLOCK, 256), f32),
            pltpu.VMEM((BLOCK, 1280), bf16),
        ],
        back,
        place_unsort,
    )
    home = exchange(unsorted.reshape(256, UNIT // 2, 2, HD), ALL).reshape(units, HD)
    return tuple(
        call(
            unpack_kernel,
            [wide, wide, narrow, narrow],
            local + [pltpu.VMEM((4, size, 2 * HD), bf16), pltpu.SemaphoreType.DMA((10,))],
            home,
            place_unpack,
            place_out=ANY,
        )
    )


def solution(mesh):
    rows = P(("inner", "outer", "head"), None)
    return jax.shard_map(
        per_device,
        mesh=mesh,
        in_specs=(rows, rows, rows, rows, P(), P()),
        out_specs=(rows, rows, rows, rows),
        check_vma=False,
    )
```

```python
import jax
import jax.numpy as jnp
from jax import lax
from jax.experimental import pallas as pl
from jax.experimental.pallas import tpu as pltpu
from jax.sharding import Mesh
from jax.sharding import PartitionSpec as P

HD = 128
GROUP = 4
KVH = 8
RUN = 128
BACK = 3
SPREAD = 32
BLOCK = 256
UNIT = 10
LOCAL = 30
SCALE = HD**-0.5
LOG2E = 1.4426950408889634
NEGATIVE = -1e30
ROWS = ("y", "z_lo", "x", "z_hi", "core")
ALL = ("z_hi", "z_lo", "y", "x", "core")
SEQ_AXES = ("y", "x", "core")
LIMIT = 48 * 1024 * 1024

f32, bf16, i32 = jnp.float32, jnp.bfloat16, jnp.int32


def iota(shape, dim):
    return lax.broadcasted_iota(i32, shape, dim)


def one_hot(condition):
    return jnp.where(condition, 1.0, 0.0).astype(bf16)


def dot(a, b):
    return jnp.dot(a, b, preferred_element_type=f32)


def dot_nt(a, b):
    return lax.dot_general(a, b, (((1,), (1,)), ((), ())), preferred_element_type=f32)


def first_row():
    device = 0
    for axis, size in zip(ROWS, (4, 2, 4, 4, 2)):
        device = device * size + lax.axis_index(axis)
    return (device * LOCAL) & (SPREAD - 1)


def seq_index():
    return lax.axis_index("y") * 8 + lax.axis_index("x") * 2 + lax.axis_index("core")


def spread_row(packed, shift):
    token = packed & 31
    to = ((shift + token) & 31) * UNIT + (packed >> 5)
    return jnp.where(token < LOCAL, to, -1)


def place_spread(rows_are_units):
    size = UNIT * 32
    to = spread_row(iota((size, size), int(rows_are_units)), first_row())
    return one_hot(iota((size, size), 1 - int(rows_are_units)) == to)


def pack_kernel(q_ref, k_ref, v_ref, g_ref, out_ref, qs, ks, vs, gs, x_ref, o_ref, in_sem, out_sem):
    size = UNIT * 32
    pairs = KVH // 2
    arrivals = []
    for i, (source, to) in enumerate(((q_ref, qs), (g_ref, gs), (k_ref, ks), (v_ref, vs))):
        arrivals.append(pltpu.make_async_copy(source, to, in_sem.at[i]))
        arrivals[-1].start()
    for u in range(UNIT):
        x_ref[pl.ds(u * 32 + 16, 16), :] = jnp.zeros((16, KVH * HD), bf16)
    place = place_spread(True)
    for copy in arrivals:
        copy.wait()
    departures = []
    for pair in range(pairs):
        for head in (2 * pair, 2 * pair + 1):
            to = pl.ds(head * HD, HD)
            for g in range(GROUP):
                column = pl.ds((head * GROUP + g) * HD, HD)
                x_ref[pl.ds(g * 32, LOCAL), to] = qs[:, column]
                x_ref[pl.ds((GROUP + g) * 32, LOCAL), to] = gs[:, column]
            x_ref[pl.ds(8 * 32, LOCAL), to] = ks[:, to]
            x_ref[pl.ds(9 * 32, LOCAL), to] = vs[:, to]
        rows = dot(place, x_ref[:, pl.ds(pair * 2 * HD, 2 * HD)]).astype(bf16)
        o_ref[pl.ds(2 * pair * size, size), :] = rows[:, :HD]
        o_ref[pl.ds((2 * pair + 1) * size, size), :] = rows[:, HD:]
        at = pl.ds(2 * pair * size, 2 * size)
        departures.append(pltpu.make_async_copy(o_ref.at[at, :], out_ref.at[at, :], out_sem.at[pair]))
        departures[-1].start()
    for copy in departures:
        copy.wait()


def unpack_kernel(r_ref, place_ref, att_ref, gq_ref, gk_ref, gv_ref, qs, ks, vs, gs, x_ref, sem):
    size = UNIT * 32
    wide, pairs = 2 * GROUP * HD, KVH // 2
    departures = []
    for pair in range(pairs):
        for half in range(2):
            x_ref[pair, :, pl.ds(half * HD, HD)] = r_ref[pl.ds((2 * pair + half) * size, size), :]
        rows = dot(place_ref[...], x_ref[pair]).astype(bf16)
        for half in range(2):
            head = 2 * pair + half
            part = rows[:, half * HD : (half + 1) * HD]
            to = pl.ds(head * HD, HD)
            for g in range(GROUP):
                column = pl.ds((head * GROUP + g) * HD, HD)
                qs[:, column] = part[g * 32 : g * 32 + LOCAL]
                gs[:, column] = part[(GROUP + g) * 32 : (GROUP + g) * 32 + LOCAL]
            ks[:, to] = part[8 * 32 : 8 * 32 + LOCAL]
            vs[:, to] = part[9 * 32 : 9 * 32 + LOCAL]
        at = pl.ds(pair * wide, wide)
        for source, to in ((qs, att_ref), (gs, gq_ref)):
            departures.append(
                pltpu.make_async_copy(source.at[:, at], to.at[:, at], sem.at[len(departures)])
            )
            departures[-1].start()
    for source, to in ((ks, gk_ref), (vs, gv_ref)):
        departures.append(pltpu.make_async_copy(source, to, sem.at[len(departures)]))
        departures[-1].start()
    for copy in departures:
        copy.wait()


def sender(run, slot, group):
    row = run * RUN + (slot & 3) * 32 + group
    device = (row * 34953) >> 20
    y, z_lo, x = device >> 6, (device >> 5) & 1, (device >> 3) & 3
    z_hi, core = (device >> 1) & 3, device & 1
    return jnp.where(run >= 0, z_hi * 64 + z_lo * 32 + y * 8 + x * 2 + core, -1)


def position(row):
    return ((row >> 2) & 1) * RUN + (row & 3) * 32 + (row >> 3)


def table_kernel(
    run_row_ref, run_col_ref, lengths_ref, sort_ref, unsort_ref, unpack_ref, begin_ref
):
    group = seq_index()
    query_pos = group * BLOCK + position(iota((1, BLOCK), 1))
    begin = jnp.zeros((1, BLOCK), i32)
    end = jnp.int32(0)
    for i in range(16):
        end = end + lengths_ref[i]
        begin = jnp.where(query_pos >= end, end, begin)
    begin_ref[...] = begin
    number = iota((BLOCK, 64), 1)
    for b in range(BACK + 1):
        slot = iota((BLOCK, 1), 0)
        found = run_row_ref[...] == (slot >> 2) - 2 * b
        run = jnp.max(jnp.where(found, number, -1), axis=1, keepdims=True)
        sort_ref[pl.ds(b * BLOCK, BLOCK), :] = one_hot(
            iota((BLOCK, BLOCK), 1) == sender(run, slot, group)
        )
    slot = iota((1, BLOCK), 1)
    found = run_col_ref[...] == (slot >> 2)
    run = jnp.max(jnp.where(found, iota((64, BLOCK), 0), -1), axis=0, keepdims=True)
    unsort_ref[...] = one_hot(iota((BLOCK, BLOCK), 0) == sender(run, slot, group))
    unpack_ref[...] = place_spread(False)


def sort_kernel(r_ref, place_ref, out_ref, wide_ref, x_ref):
    wide_ref[...] = r_ref[...].astype(f32)
    for u in range(UNIT):
        x_ref[:, pl.ds(u * HD, HD)] = wide_ref[pl.ds(u, BLOCK, stride=UNIT), :].astype(bf16)
    out_ref[:, pl.ds(0, 1280)] = dot(place_ref[pl.ds(0, BLOCK), :], x_ref[...]).astype(bf16)
    for b in range(1, BACK + 1):
        out_ref[:, pl.ds(1024 + 256 * b, 256)] = dot(
            place_ref[pl.ds(b * BLOCK, BLOCK), :], x_ref[:, pl.ds(1024, 256)]
        ).astype(bf16)


def unsort_kernel(r_ref, place_ref, out_ref, wide_ref, sum_ref, x_ref):
    for b in range(BACK + 1):
        part = r_ref[b:SPREAD, :, pl.ds(1024 + 256 * b, 256)].astype(f32)
        part = part.reshape((SPREAD - b) * 8, 256)
        rows = pl.ds(0, (SPREAD - b) * 8)
        if b == 0:
            sum_ref[rows, :] = part
        else:
            sum_ref[rows, :] = sum_ref[rows, :] + part
    x_ref[:, pl.ds(0, 1024)] = r_ref[:, :, pl.ds(0, 1024)].reshape(BLOCK, 1024)
    x_ref[:, pl.ds(1024, 256)] = sum_ref[...].astype(bf16)
    for pair in range(UNIT // 2):
        rows = dot(place_ref[...], x_ref[:, pl.ds(pair * 2 * HD, 2 * HD)])
        wide_ref[pl.ds(2 * pair, BLOCK, stride=UNIT), :] = rows[:, :HD]
        wide_ref[pl.ds(2 * pair + 1, BLOCK, stride=UNIT), :] = rows[:, HD:]
    out_ref[...] = wide_ref[...].astype(bf16)


def attention_kernel(
    begin_ref, m_ref, out_ref, bias_ref, s_ref, dp_ref, p_ref, d_ref, q_ref, g_ref, k_ref, v_ref,
):
    base = seq_index() * BLOCK
    blocks, heads = range(BACK + 1), range(GROUP)

    def rows(b):
        return pl.ds(b * BLOCK, BLOCK)

    query_pos = base + position(iota((1, BLOCK), 1))
    begin = begin_ref[...]
    key_pos = base + position(iota((BLOCK, BLOCK), 0))
    for b in blocks:
        seen = key_pos >= begin + b * BLOCK
        if b == 0:
            seen = seen & (key_pos <= query_pos)
        bias_ref[rows(b), :] = jnp.where(seen, 0.0, NEGATIVE)
        k_ref[rows(b), :] = m_ref[:, pl.ds(1024 + 256 * b, HD)]
        v_ref[rows(b), :] = m_ref[:, pl.ds(1024 + 256 * b + HD, HD)]
    for g in heads:
        q_ref[rows(g), :] = m_ref[:, pl.ds(g * HD, HD)]
        g_ref[rows(g), :] = m_ref[:, pl.ds((GROUP + g) * HD, HD)]
    keys, values = k_ref[...], v_ref[...]
    keys_t, values_t = keys.T, values.T

    tops, inverses, deltas = [], [], []
    for g in heads:
        s = dot_nt(keys, q_ref[rows(g), :]) * (SCALE * LOG2E) + bias_ref[...]
        s_ref[:, rows(g)] = s
        tops.append(jnp.max(s, axis=0, keepdims=True))
        dp_ref[:, rows(g)] = dot_nt(values, g_ref[rows(g), :])
    for g in heads:
        weights = jnp.exp2(s_ref[:, rows(g)] - tops[g])
        s_ref[:, rows(g)] = weights
        inverse = 1.0 / jnp.sum(weights, axis=0, keepdims=True)
        output = (dot(values_t, weights.astype(bf16)) * inverse).T.astype(bf16)
        out_ref[:, pl.ds(g * HD, HD)] = output
        product = g_ref[rows(g), :].astype(f32) * output.astype(f32)
        deltas.append(jnp.sum(product.T, axis=0, keepdims=True))
        inverses.append(inverse)
    for g in heads:
        prob = s_ref[:, rows(g)] * inverses[g]
        p_ref[:, rows(g)] = prob.astype(bf16)
        dscore = (prob * (dp_ref[:, rows(g)] - deltas[g])).astype(bf16)
        d_ref[:, rows(g)] = dscore
        out_ref[:, pl.ds((GROUP + g) * HD, HD)] = (dot(keys_t, dscore) * SCALE).T.astype(bf16)
    for b in blocks:
        at = 2 * GROUP * HD + 2 * HD * b
        out_ref[:, pl.ds(at, HD)] = (dot(d_ref[rows(b), :], q_ref[...]) * SCALE).astype(bf16)
        out_ref[:, pl.ds(at + HD, HD)] = dot(p_ref[rows(b), :], g_ref[...]).astype(bf16)


VMEM = pl.BlockSpec(memory_space=pltpu.VMEM)
ANY = pl.BlockSpec(memory_space=pl.ANY)


def call(kernel, outs, scratch, *args, place_in=VMEM, place_out=VMEM, limit=LIMIT):
    return pl.pallas_call(
        kernel,
        out_shape=[jax.ShapeDtypeStruct(o, bf16) for o in outs],
        in_specs=[place_in] * len(args),
        out_specs=[place_out] * len(outs),
        scratch_shapes=scratch,
        compiler_params=pltpu.CompilerParams(vmem_limit_bytes=limit),
    )(*args)


def exchange(x, axes):
    return lax.all_to_all(x, axes, split_axis=0, concat_axis=0, tiled=True)


def per_device(queries, keys, values, grad_out, doc_lengths, positions):
    units, size = 256 * UNIT, UNIT * 32
    wide, narrow = (LOCAL, KVH * GROUP * HD), (LOCAL, KVH * HD)
    local = [pltpu.VMEM(s, bf16) for s in (wide, narrow, narrow, wide)]
    runs = jnp.pad(positions[::RUN] // RUN, (0, 4), constant_values=-1000)
    table = pl.pallas_call(
        table_kernel,
        out_shape=[
            jax.ShapeDtypeStruct(((BACK + 1) * BLOCK, BLOCK), bf16),
            jax.ShapeDtypeStruct((BLOCK, BLOCK), bf16),
            jax.ShapeDtypeStruct((size, size), bf16),
            jax.ShapeDtypeStruct((1, BLOCK), i32),
        ],
        in_specs=[VMEM, VMEM, pl.BlockSpec(memory_space=pltpu.SMEM)],
        out_specs=[VMEM] * 4,
        compiler_params=pltpu.CompilerParams(vmem_limit_bytes=LIMIT),
        cost_estimate=pl.CostEstimate(flops=1 << 24, bytes_accessed=1 << 18, transcendentals=0),
    )
    place_sort, place_unsort, place_unpack, begin = table(
        runs.reshape(1, 64), runs.reshape(64, 1), doc_lengths
    )
    (packed,) = call(
        pack_kernel,
        [(units, HD)],
        local
        + [
            pltpu.VMEM((size, KVH * HD), bf16),
            pltpu.VMEM((units, HD), bf16),
            pltpu.SemaphoreType.DMA((4,)),
            pltpu.SemaphoreType.DMA((4,)),
        ],
        queries,
        keys,
        values,
        grad_out,
        place_in=ANY,
        limit=None,
        place_out=ANY,
    )
    spread = exchange(packed.reshape(256, UNIT // 2, 2, HD), ALL).reshape(units, HD)
    (ordered,) = call(
        sort_kernel,
        [(BLOCK, 2048)],
        [pltpu.VMEM((units, HD), f32), pltpu.VMEM((BLOCK, 1280), bf16)],
        spread,
        place_sort,
    )
    block = exchange(ordered.reshape(SPREAD, 8, 2048), SEQ_AXES).reshape(BLOCK, 2048)
    square = (GROUP * BLOCK, (BACK + 1) * BLOCK)
    (done,) = call(
        attention_kernel,
        [(BLOCK, 2048)],
        [
            pltpu.VMEM((square[1], BLOCK), f32),
            pltpu.VMEM(square, f32),
            pltpu.VMEM(square, f32),
            pltpu.VMEM(square, bf16),
            pltpu.VMEM(square, bf16),
        ]
        + [pltpu.VMEM((square[0], HD), bf16)] * 4,
        begin,
        block,
    )
    back = exchange(done.reshape(SPREAD, 8, 2048), SEQ_AXES)
    (unsorted,) = call(
        unsort_kernel,
        [(units, HD)],
        [
            pltpu.VMEM((units, HD), f32),
            pltpu.VMEM((BLOCK, 256), f32),
            pltpu.VMEM((BLOCK, 1280), bf16),
        ],
        back,
        place_unsort,
    )
    home = exchange(unsorted.reshape(256, UNIT // 2, 2, HD), ALL).reshape(units, HD)
    return tuple(
        call(
            unpack_kernel,
            [wide, wide, narrow, narrow],
            local + [pltpu.VMEM((4, size, 2 * HD), bf16), pltpu.SemaphoreType.DMA((10,))],
            home,
            place_unpack,
            place_out=ANY,
        )
    )


def solution(mesh):
    parts = {"head": (("z_hi", 4), ("core", 2)), "inner": (("y", 4),), "outer": (("z_lo", 2), ("x", 4))}
    axes = [part for name in mesh.axis_names for part in parts[name]]
    split = Mesh(mesh.devices.reshape([size for _, size in axes]), [name for name, _ in axes])
    rows = P(ROWS, None)
    return jax.shard_map(
        per_device,
        mesh=split,
        in_specs=(rows, rows, rows, rows, P(), P()),
        out_specs=(rows, rows, rows, rows),
        check_vma=False,
    )
```

```python
import jax
import jax.numpy as jnp
from jax import lax
from jax.experimental import pallas as pl
from jax.experimental.pallas import tpu as pltpu
from jax.sharding import Mesh
from jax.sharding import PartitionSpec as P

HD = 128
GROUP = 4
KVH = 8
RUN = 128
BACK = 3
SPREAD = 32
BLOCK = 256
UNIT = 10
LOCAL = 30
SCALE = HD**-0.5
LOG2E = 1.4426950408889634
NEGATIVE = -1e30
ROWS = ("y", "z_lo", "x", "z_hi", "core")
ALL = ("z_hi", "z_lo", "y", "x", "core")
SEQ_AXES = ("y", "x", "core")
LIMIT = 48 * 1024 * 1024

f32, bf16, i32 = jnp.float32, jnp.bfloat16, jnp.int32


def iota(shape, dim):
    return lax.broadcasted_iota(i32, shape, dim)


def one_hot(condition):
    return jnp.where(condition, 1.0, 0.0).astype(bf16)


def dot(a, b):
    return jnp.dot(a, b, preferred_element_type=f32)


def dot_nt(a, b):
    return lax.dot_general(a, b, (((1,), (1,)), ((), ())), preferred_element_type=f32)


def first_row():
    device = 0
    for axis, size in zip(ROWS, (4, 2, 4, 4, 2)):
        device = device * size + lax.axis_index(axis)
    return (device * LOCAL) & (SPREAD - 1)


def seq_index():
    return lax.axis_index("y") * 8 + lax.axis_index("x") * 2 + lax.axis_index("core")


def spread_row(packed, shift):
    token = packed & 31
    to = ((shift + token) & 31) * UNIT + (packed >> 5)
    return jnp.where(token < LOCAL, to, -1)


def place_spread(rows_are_units):
    size = UNIT * 32
    to = spread_row(iota((size, size), int(rows_are_units)), first_row())
    return one_hot(iota((size, size), 1 - int(rows_are_units)) == to)


def pack_kernel(q_ref, k_ref, v_ref, g_ref, out_ref, qs, ks, vs, gs, x_ref, o_ref, in_sem, out_sem):
    size = UNIT * 32
    pairs = KVH // 2
    arrivals = []
    for i, (source, to) in enumerate(((q_ref, qs), (g_ref, gs), (k_ref, ks), (v_ref, vs))):
        arrivals.append(pltpu.make_async_copy(source, to, in_sem.at[i]))
        arrivals[-1].start()
    for u in range(UNIT):
        x_ref[pl.ds(u * 32 + 16, 16), :] = jnp.zeros((16, KVH * HD), bf16)
    place = place_spread(True)
    for copy in arrivals:
        copy.wait()
    departures = []
    for pair in range(pairs):
        for head in (2 * pair, 2 * pair + 1):
            to = pl.ds(head * HD, HD)
            for g in range(GROUP):
                column = pl.ds((head * GROUP + g) * HD, HD)
                x_ref[pl.ds(g * 32, LOCAL), to] = qs[:, column]
                x_ref[pl.ds((GROUP + g) * 32, LOCAL), to] = gs[:, column]
            x_ref[pl.ds(8 * 32, LOCAL), to] = ks[:, to]
            x_ref[pl.ds(9 * 32, LOCAL), to] = vs[:, to]
        rows = dot(place, x_ref[:, pl.ds(pair * 2 * HD, 2 * HD)]).astype(bf16)
        o_ref[pl.ds(2 * pair * size, size), :] = rows[:, :HD]
        o_ref[pl.ds((2 * pair + 1) * size, size), :] = rows[:, HD:]
        at = pl.ds(2 * pair * size, 2 * size)
        departures.append(pltpu.make_async_copy(o_ref.at[at, :], out_ref.at[at, :], out_sem.at[pair]))
        departures[-1].start()
    for copy in departures:
        copy.wait()


def unpack_kernel(r_ref, place_ref, att_ref, gq_ref, gk_ref, gv_ref, qs, ks, vs, gs, x_ref, sem):
    size = UNIT * 32
    wide, pairs = 2 * GROUP * HD, KVH // 2
    departures = []
    for pair in range(pairs):
        for half in range(2):
            x_ref[pair, :, pl.ds(half * HD, HD)] = r_ref[pl.ds((2 * pair + half) * size, size), :]
        rows = dot(place_ref[...], x_ref[pair]).astype(bf16)
        for half in range(2):
            head = 2 * pair + half
            part = rows[:, half * HD : (half + 1) * HD]
            to = pl.ds(head * HD, HD)
            for g in range(GROUP):
                column = pl.ds((head * GROUP + g) * HD, HD)
                qs[:, column] = part[g * 32 : g * 32 + LOCAL]
                gs[:, column] = part[(GROUP + g) * 32 : (GROUP + g) * 32 + LOCAL]
            ks[:, to] = part[8 * 32 : 8 * 32 + LOCAL]
            vs[:, to] = part[9 * 32 : 9 * 32 + LOCAL]
        at = pl.ds(pair * wide, wide)
        for source, to in ((qs, att_ref), (gs, gq_ref)):
            departures.append(
                pltpu.make_async_copy(source.at[:, at], to.at[:, at], sem.at[len(departures)])
            )
            departures[-1].start()
    for source, to in ((ks, gk_ref), (vs, gv_ref)):
        departures.append(pltpu.make_async_copy(source, to, sem.at[len(departures)]))
        departures[-1].start()
    for copy in departures:
        copy.wait()


def sender(run, slot, group):
    row = run * RUN + (slot & 3) * 32 + group
    device = (row * 34953) >> 20
    y, z_lo, x = device >> 6, (device >> 5) & 1, (device >> 3) & 3
    z_hi, core = (device >> 1) & 3, device & 1
    return jnp.where(run >= 0, z_hi * 64 + z_lo * 32 + y * 8 + x * 2 + core, -1)


def position(row):
    return ((row >> 2) & 1) * RUN + (row & 3) * 32 + (row >> 3)


def table_kernel(
    run_row_ref, run_col_ref, lengths_ref, sort_ref, unsort_ref, unpack_ref, begin_ref
):
    group = seq_index()
    query_pos = group * BLOCK + position(iota((1, BLOCK), 1))
    begin = jnp.zeros((1, BLOCK), i32)
    end = jnp.int32(0)
    for i in range(16):
        end = end + lengths_ref[i]
        begin = jnp.where(query_pos >= end, end, begin)
    begin_ref[...] = begin
    number = iota((BLOCK, 64), 1)
    for b in range(BACK + 1):
        slot = iota((BLOCK, 1), 0)
        found = run_row_ref[...] == (slot >> 2) - 2 * b
        run = jnp.max(jnp.where(found, number, -1), axis=1, keepdims=True)
        sort_ref[pl.ds(b * BLOCK, BLOCK), :] = one_hot(
            iota((BLOCK, BLOCK), 1) == sender(run, slot, group)
        )
    slot = iota((1, BLOCK), 1)
    found = run_col_ref[...] == (slot >> 2)
    run = jnp.max(jnp.where(found, iota((64, BLOCK), 0), -1), axis=0, keepdims=True)
    unsort_ref[...] = one_hot(iota((BLOCK, BLOCK), 0) == sender(run, slot, group))
    unpack_ref[...] = place_spread(False)


def sort_kernel(r_ref, place_ref, out_ref, wide_ref, x_ref):
    wide_ref[pl.ds(0, UNIT * BLOCK), :] = r_ref[...].astype(f32)
    for u in range(UNIT):
        x_ref[:, pl.ds(u * HD, HD)] = wide_ref[pl.ds(u, BLOCK, stride=UNIT), :].astype(bf16)
    out_ref[:, pl.ds(0, 1280)] = dot(place_ref[pl.ds(0, BLOCK), :], x_ref[...]).astype(bf16)
    for b in range(1, BACK + 1):
        out_ref[:, pl.ds(1024 + 256 * b, 256)] = dot(
            place_ref[pl.ds(b * BLOCK, BLOCK), :], x_ref[:, pl.ds(1024, 256)]
        ).astype(bf16)


def unsort_kernel(r_ref, place_ref, out_ref, wide_ref, sum_ref, x_ref):
    for b in range(BACK + 1):
        part = r_ref[b:SPREAD, :, pl.ds(1024 + 256 * b, 256)].astype(f32)
        part = part.reshape((SPREAD - b) * 8, 256)
        rows = pl.ds(0, (SPREAD - b) * 8)
        if b == 0:
            sum_ref[rows, :] = part
        else:
            sum_ref[rows, :] = sum_ref[rows, :] + part
    x_ref[:, pl.ds(0, 1024)] = r_ref[:, :, pl.ds(0, 1024)].reshape(BLOCK, 1024)
    x_ref[:, pl.ds(1024, 256)] = sum_ref[...].astype(bf16)
    for pair in range(UNIT // 2):
        rows = dot(place_ref[...], x_ref[:, pl.ds(pair * 2 * HD, 2 * HD)])
        wide_ref[pl.ds(2 * pair, BLOCK, stride=UNIT), :] = rows[:, :HD]
        wide_ref[pl.ds(2 * pair + 1, BLOCK, stride=UNIT), :] = rows[:, HD:]
    out_ref[...] = wide_ref[pl.ds(0, UNIT * BLOCK), :].astype(bf16)


def attention_kernel(
    begin_ref, m_ref, out_ref, bias_ref, s_ref, dp_ref, p_ref, d_ref, q_ref, g_ref, k_ref, v_ref,
):
    base = seq_index() * BLOCK
    blocks, heads = range(BACK + 1), range(GROUP)

    def rows(b):
        return pl.ds(b * BLOCK, BLOCK)

    query_pos = base + position(iota((1, BLOCK), 1))
    begin = begin_ref[...]
    key_pos = base + position(iota((BLOCK, BLOCK), 0))
    for b in blocks:
        seen = key_pos >= begin + b * BLOCK
        if b == 0:
            seen = seen & (key_pos <= query_pos)
        bias_ref[rows(b), :] = jnp.where(seen, 0.0, NEGATIVE)
        k_ref[rows(b), :] = m_ref[:, pl.ds(1024 + 256 * b, HD)]
        v_ref[rows(b), :] = m_ref[:, pl.ds(1024 + 256 * b + HD, HD)]
    for g in heads:
        q_ref[rows(g), :] = m_ref[:, pl.ds(g * HD, HD)]
        g_ref[rows(g), :] = m_ref[:, pl.ds((GROUP + g) * HD, HD)]
    keys, values = k_ref[...], v_ref[...]
    keys_t, values_t = keys.T, values.T

    tops, accums, inverses, deltas = [], [], [], []
    for g in heads:
        s = dot_nt(keys, q_ref[rows(g), :]) * (SCALE * LOG2E) + bias_ref[...]
        s_ref[:, rows(g)] = s
        tops.append(jnp.max(s, axis=0, keepdims=True))
    for g in heads:
        weights = jnp.exp2(s_ref[:, rows(g)] - tops[g])
        s_ref[:, rows(g)] = weights
        inverses.append(1.0 / jnp.sum(weights, axis=0, keepdims=True))
        accums.append(dot(values_t, weights.astype(bf16)))
        dp_ref[:, rows(g)] = dot_nt(values, g_ref[rows(g), :])
    for g in heads:
        output = (accums[g] * inverses[g]).T.astype(bf16)
        out_ref[:, pl.ds(g * HD, HD)] = output
        product = g_ref[rows(g), :].astype(f32) * output.astype(f32)
        deltas.append(jnp.sum(product.T, axis=0, keepdims=True))
    for g in heads:
        prob = s_ref[:, rows(g)] * inverses[g]
        p_ref[:, rows(g)] = prob.astype(bf16)
        dscore = (prob * (dp_ref[:, rows(g)] - deltas[g])).astype(bf16)
        d_ref[:, rows(g)] = dscore
        out_ref[:, pl.ds((GROUP + g) * HD, HD)] = (dot(keys_t, dscore) * SCALE).T.astype(bf16)
    for b in blocks:
        at = 2 * GROUP * HD + 2 * HD * b
        out_ref[:, pl.ds(at, HD)] = (dot(d_ref[rows(b), :], q_ref[...]) * SCALE).astype(bf16)
        out_ref[:, pl.ds(at + HD, HD)] = dot(p_ref[rows(b), :], g_ref[...]).astype(bf16)


VMEM = pl.BlockSpec(memory_space=pltpu.VMEM)
ANY = pl.BlockSpec(memory_space=pl.ANY)


def call(kernel, outs, scratch, *args, place_in=VMEM, place_out=VMEM, limit=LIMIT):
    return pl.pallas_call(
        kernel,
        out_shape=[jax.ShapeDtypeStruct(o, bf16) for o in outs],
        in_specs=[place_in] * len(args),
        out_specs=[place_out] * len(outs),
        scratch_shapes=scratch,
        compiler_params=pltpu.CompilerParams(vmem_limit_bytes=limit),
    )(*args)


def exchange(x, axes):
    return lax.all_to_all(x, axes, split_axis=0, concat_axis=0, tiled=True)


def per_device(queries, keys, values, grad_out, doc_lengths, positions):
    units, size = 256 * UNIT, UNIT * 32
    wide, narrow = (LOCAL, KVH * GROUP * HD), (LOCAL, KVH * HD)
    local = [pltpu.VMEM(s, bf16) for s in (wide, narrow, narrow, wide)]
    runs = jnp.pad(positions[::RUN] // RUN, (0, 4), constant_values=-1000)
    table = pl.pallas_call(
        table_kernel,
        out_shape=[
            jax.ShapeDtypeStruct(((BACK + 1) * BLOCK, BLOCK), bf16),
            jax.ShapeDtypeStruct((BLOCK, BLOCK), bf16),
            jax.ShapeDtypeStruct((size, size), bf16),
            jax.ShapeDtypeStruct((1, BLOCK), i32),
        ],
        in_specs=[VMEM, VMEM, pl.BlockSpec(memory_space=pltpu.SMEM)],
        out_specs=[VMEM] * 4,
        compiler_params=pltpu.CompilerParams(vmem_limit_bytes=LIMIT),
        cost_estimate=pl.CostEstimate(flops=1 << 24, bytes_accessed=1 << 18, transcendentals=0),
    )
    place_sort, place_unsort, place_unpack, begin = table(
        runs.reshape(1, 64), runs.reshape(64, 1), doc_lengths
    )
    (packed,) = call(
        pack_kernel,
        [(units, HD)],
        local
        + [
            pltpu.VMEM((size, KVH * HD), bf16),
            pltpu.VMEM((units, HD), bf16),
            pltpu.SemaphoreType.DMA((4,)),
            pltpu.SemaphoreType.DMA((4,)),
        ],
        queries,
        keys,
        values,
        grad_out,
        place_in=ANY,
        limit=None,
        place_out=ANY,
    )
    spread = exchange(packed.reshape(256, UNIT // 2, 2, HD), ALL).reshape(units, HD)
    (ordered,) = call(
        sort_kernel,
        [(BLOCK, 2048)],
        [pltpu.VMEM((units + 16, HD), f32), pltpu.VMEM((BLOCK, 1280), bf16)],
        spread,
        place_sort,
    )
    block = exchange(ordered.reshape(SPREAD, 8, 2048), SEQ_AXES).reshape(BLOCK, 2048)
    square = (GROUP * BLOCK, (BACK + 1) * BLOCK)
    (done,) = call(
        attention_kernel,
        [(BLOCK, 2048)],
        [
            pltpu.VMEM((square[1], BLOCK), f32),
            pltpu.VMEM(square, f32),
            pltpu.VMEM(square, f32),
            pltpu.VMEM(square, bf16),
            pltpu.VMEM(square, bf16),
        ]
        + [pltpu.VMEM((square[0], HD), bf16)] * 4,
        begin,
        block,
    )
    back = exchange(done.reshape(SPREAD, 8, 2048), SEQ_AXES)
    (unsorted,) = call(
        unsort_kernel,
        [(units, HD)],
        [
            pltpu.VMEM((units + 16, HD), f32),
            pltpu.VMEM((BLOCK, 256), f32),
            pltpu.VMEM((BLOCK, 1280), bf16),
        ],
        back,
        place_unsort,
    )
    home = exchange(unsorted.reshape(256, UNIT // 2, 2, HD), ALL).reshape(units, HD)
    return tuple(
        call(
            unpack_kernel,
            [wide, wide, narrow, narrow],
            local + [pltpu.VMEM((4, size, 2 * HD), bf16), pltpu.SemaphoreType.DMA((10,))],
            home,
            place_unpack,
            place_out=ANY,
        )
    )


def solution(mesh):
    parts = {"head": (("z_hi", 4), ("core", 2)), "inner": (("y", 4),), "outer": (("z_lo", 2), ("x", 4))}
    axes = [part for name in mesh.axis_names for part in parts[name]]
    split = Mesh(mesh.devices.reshape([size for _, size in axes]), [name for name, _ in axes])
    rows = P(ROWS, None)
    return jax.shard_map(
        per_device,
        mesh=split,
        in_specs=(rows, rows, rows, rows, P(), P()),
        out_specs=(rows, rows, rows, rows),
        check_vma=False,
    )
```

```python
import jax
import jax.numpy as jnp
from jax import lax
from jax.experimental import pallas as pl
from jax.experimental.pallas import tpu as pltpu
from jax.sharding import Mesh
from jax.sharding import PartitionSpec as P

HD = 128
GROUP = 4
KVH = 8
RUN = 128
BACK = 3
SPREAD = 32
BLOCK = 256
UNIT = 10
LOCAL = 30
SCALE = HD**-0.5
LOG2E = 1.4426950408889634
NEGATIVE = -1e30
ROWS = ("y", "z_lo", "x", "z_hi", "core")
ALL = ("z_hi", "z_lo", "y", "x", "core")
SEQ_AXES = ("y", "x", "core")
LIMIT = 48 * 1024 * 1024

f32, bf16, i32 = jnp.float32, jnp.bfloat16, jnp.int32


def iota(shape, dim):
    return lax.broadcasted_iota(i32, shape, dim)


def one_hot(condition):
    return jnp.where(condition, 1.0, 0.0).astype(bf16)


def dot(a, b):
    return jnp.dot(a, b, preferred_element_type=f32)


def dot_nt(a, b):
    return lax.dot_general(a, b, (((1,), (1,)), ((), ())), preferred_element_type=f32)


def first_row():
    device = 0
    for axis, size in zip(ROWS, (4, 2, 4, 4, 2)):
        device = device * size + lax.axis_index(axis)
    return (device * LOCAL) & (SPREAD - 1)


def seq_index():
    return lax.axis_index("y") * 8 + lax.axis_index("x") * 2 + lax.axis_index("core")


def spread_row(packed, shift):
    token = packed & 31
    to = ((shift + token) & 31) * UNIT + (packed >> 5)
    return jnp.where(token < LOCAL, to, -1)


def place_spread(rows_are_units):
    size = UNIT * 32
    to = spread_row(iota((size, size), int(rows_are_units)), first_row())
    return one_hot(iota((size, size), 1 - int(rows_are_units)) == to)


def pack_kernel(q_ref, k_ref, v_ref, g_ref, out_ref, qs, ks, vs, gs, x_ref, o_ref, in_sem, out_sem):
    size = UNIT * 32
    pairs = KVH // 2
    arrivals = []
    for i, (source, to) in enumerate(((q_ref, qs), (g_ref, gs), (k_ref, ks), (v_ref, vs))):
        arrivals.append(pltpu.make_async_copy(source, to, in_sem.at[i]))
        arrivals[-1].start()
    for u in range(UNIT):
        x_ref[pl.ds(u * 32 + 16, 16), :] = jnp.zeros((16, KVH * HD), bf16)
    place = place_spread(True)
    for copy in arrivals:
        copy.wait()
    departures = []
    for pair in range(pairs):
        for head in (2 * pair, 2 * pair + 1):
            to = pl.ds(head * HD, HD)
            for g in range(GROUP):
                column = pl.ds((head * GROUP + g) * HD, HD)
                x_ref[pl.ds(g * 32, LOCAL), to] = qs[:, column]
                x_ref[pl.ds((GROUP + g) * 32, LOCAL), to] = gs[:, column]
            x_ref[pl.ds(8 * 32, LOCAL), to] = ks[:, to]
            x_ref[pl.ds(9 * 32, LOCAL), to] = vs[:, to]
        rows = dot(place, x_ref[:, pl.ds(pair * 2 * HD, 2 * HD)]).astype(bf16)
        o_ref[pl.ds(2 * pair * size, size), :] = rows[:, :HD]
        o_ref[pl.ds((2 * pair + 1) * size, size), :] = rows[:, HD:]
        at = pl.ds(2 * pair * size, 2 * size)
        departures.append(pltpu.make_async_copy(o_ref.at[at, :], out_ref.at[at, :], out_sem.at[pair]))
        departures[-1].start()
    for copy in departures:
        copy.wait()


def unpack_kernel(r_ref, place_ref, att_ref, gq_ref, gk_ref, gv_ref, qs, ks, vs, gs, x_ref, sem):
    size = UNIT * 32
    wide, pairs = 2 * GROUP * HD, KVH // 2
    departures = []
    for pair in range(pairs):
        for half in range(2):
            x_ref[pair, :, pl.ds(half * HD, HD)] = r_ref[pl.ds((2 * pair + half) * size, size), :]
        rows = dot(place_ref[...], x_ref[pair]).astype(bf16)
        for half in range(2):
            head = 2 * pair + half
            part = rows[:, half * HD : (half + 1) * HD]
            to = pl.ds(head * HD, HD)
            for g in range(GROUP):
                column = pl.ds((head * GROUP + g) * HD, HD)
                qs[:, column] = part[g * 32 : g * 32 + LOCAL]
                gs[:, column] = part[(GROUP + g) * 32 : (GROUP + g) * 32 + LOCAL]
            ks[:, to] = part[8 * 32 : 8 * 32 + LOCAL]
            vs[:, to] = part[9 * 32 : 9 * 32 + LOCAL]
        at = pl.ds(pair * wide, wide)
        for source, to in ((qs, att_ref), (gs, gq_ref)):
            departures.append(
                pltpu.make_async_copy(source.at[:, at], to.at[:, at], sem.at[len(departures)])
            )
            departures[-1].start()
    for source, to in ((ks, gk_ref), (vs, gv_ref)):
        departures.append(pltpu.make_async_copy(source, to, sem.at[len(departures)]))
        departures[-1].start()
    for copy in departures:
        copy.wait()


def sender(run, slot, group):
    row = run * RUN + (slot & 3) * 32 + group
    device = (row * 34953) >> 20
    y, z_lo, x = device >> 6, (device >> 5) & 1, (device >> 3) & 3
    z_hi, core = (device >> 1) & 3, device & 1
    return jnp.where(run >= 0, z_hi * 64 + z_lo * 32 + y * 8 + x * 2 + core, -1)


def position(row):
    return ((row >> 2) & 1) * RUN + (row & 3) * 32 + (row >> 3)


def table_kernel(
    run_row_ref, run_col_ref, lengths_ref, sort_ref, unsort_ref, unpack_ref, begin_ref
):
    group = seq_index()
    query_pos = group * BLOCK + position(iota((1, BLOCK), 1))
    begin = jnp.zeros((1, BLOCK), i32)
    end = jnp.int32(0)
    for i in range(16):
        end = end + lengths_ref[i]
        begin = jnp.where(query_pos >= end, end, begin)
    begin_ref[...] = begin
    number = iota((BLOCK, 64), 1)
    for b in range(BACK + 1):
        slot = iota((BLOCK, 1), 0)
        found = run_row_ref[...] == (slot >> 2) - 2 * b
        run = jnp.max(jnp.where(found, number, -1), axis=1, keepdims=True)
        sort_ref[pl.ds(b * BLOCK, BLOCK), :] = one_hot(
            iota((BLOCK, BLOCK), 1) == sender(run, slot, group)
        )
    slot = iota((1, BLOCK), 1)
    found = run_col_ref[...] == (slot >> 2)
    run = jnp.max(jnp.where(found, iota((64, BLOCK), 0), -1), axis=0, keepdims=True)
    unsort_ref[...] = one_hot(iota((BLOCK, BLOCK), 0) == sender(run, slot, group))
    unpack_ref[...] = place_spread(False)


def sort_kernel(r_ref, place_ref, out_ref, wide_ref, x_ref):
    wide_ref[pl.ds(0, UNIT * BLOCK), :] = r_ref[...].astype(f32)
    for u in range(UNIT):
        x_ref[:, pl.ds(u * HD, HD)] = wide_ref[pl.ds(u, BLOCK, stride=UNIT), :].astype(bf16)
    out_ref[:, pl.ds(0, 1280)] = dot(place_ref[pl.ds(0, BLOCK), :], x_ref[...]).astype(bf16)
    for b in range(1, BACK + 1):
        out_ref[:, pl.ds(1024 + 256 * b, 256)] = dot(
            place_ref[pl.ds(b * BLOCK, BLOCK), :], x_ref[:, pl.ds(1024, 256)]
        ).astype(bf16)


def unsort_kernel(r_ref, place_ref, out_ref, wide_ref, sum_ref, x_ref):
    for b in range(BACK + 1):
        part = r_ref[b:SPREAD, :, pl.ds(1024 + 256 * b, 256)].astype(f32)
        part = part.reshape((SPREAD - b) * 8, 256)
        rows = pl.ds(0, (SPREAD - b) * 8)
        if b == 0:
            sum_ref[rows, :] = part
        else:
            sum_ref[rows, :] = sum_ref[rows, :] + part
    x_ref[:, pl.ds(0, 1024)] = r_ref[:, :, pl.ds(0, 1024)].reshape(BLOCK, 1024)
    x_ref[:, pl.ds(1024, 256)] = sum_ref[...].astype(bf16)
    for pair in range(UNIT // 2):
        rows = dot(place_ref[...], x_ref[:, pl.ds(pair * 2 * HD, 2 * HD)])
        wide_ref[pl.ds(2 * pair, BLOCK, stride=UNIT), :] = rows[:, :HD]
        wide_ref[pl.ds(2 * pair + 1, BLOCK, stride=UNIT), :] = rows[:, HD:]
    out_ref[...] = wide_ref[pl.ds(0, UNIT * BLOCK), :].astype(bf16)


def attention_kernel(
    begin_ref, m_ref, out_ref, bias_ref, s_ref, dp_ref, p_ref, d_ref, q_ref, g_ref, k_ref, v_ref,
    dk_ref, dv_ref,
):
    base = seq_index() * BLOCK
    blocks, heads = range(BACK + 1), range(GROUP)

    def rows(b):
        return pl.ds(b * BLOCK, BLOCK)

    query_pos = base + position(iota((1, BLOCK), 1))
    begin = begin_ref[...]
    key_pos = base + position(iota((BLOCK, BLOCK), 0))
    for b in blocks:
        seen = key_pos >= begin + b * BLOCK
        if b == 0:
            seen = seen & (key_pos <= query_pos)
        bias_ref[rows(b), :] = jnp.where(seen, 0.0, NEGATIVE)
        k_ref[rows(b), :] = m_ref[:, pl.ds(1024 + 256 * b, HD)]
        v_ref[rows(b), :] = m_ref[:, pl.ds(1024 + 256 * b + HD, HD)]
    for g in heads:
        q_ref[rows(g), :] = m_ref[:, pl.ds(g * HD, HD)]
        g_ref[rows(g), :] = m_ref[:, pl.ds((GROUP + g) * HD, HD)]
    keys, values = k_ref[...], v_ref[...]
    keys_t, values_t = keys.T, values.T

    tops, accums, inverses, deltas = {}, {}, {}, {}

    def score(g):
        s = dot_nt(keys, q_ref[rows(g), :]) * (SCALE * LOG2E) + bias_ref[...]
        s_ref[:, rows(g)] = s
        tops[g] = jnp.max(s, axis=0, keepdims=True)

    def weigh(g):
        weights = jnp.exp2(s_ref[:, rows(g)] - tops[g])
        s_ref[:, rows(g)] = weights
        inverses[g] = 1.0 / jnp.sum(weights, axis=0, keepdims=True)
        accums[g] = dot(values_t, weights.astype(bf16))
        dp_ref[:, rows(g)] = dot_nt(values, g_ref[rows(g), :])

    def attend(g):
        output = (accums[g] * inverses[g]).T.astype(bf16)
        out_ref[:, pl.ds(g * HD, HD)] = output
        product = g_ref[rows(g), :].astype(f32) * output.astype(f32)
        deltas[g] = jnp.sum(product.T, axis=0, keepdims=True)

    def back(g):
        prob = s_ref[:, rows(g)] * inverses[g]
        p_ref[:, rows(g)] = prob.astype(bf16)
        dscore = (prob * (dp_ref[:, rows(g)] - deltas[g])).astype(bf16)
        d_ref[:, rows(g)] = dscore
        out_ref[:, pl.ds((GROUP + g) * HD, HD)] = (dot(keys_t, dscore) * SCALE).T.astype(bf16)

    def key_grads(half):
        two = pl.ds(half * 2 * BLOCK, 2 * BLOCK)
        for b in blocks:
            key_term = dot(d_ref[rows(b), two], q_ref[two, :])
            value_term = dot(p_ref[rows(b), two], g_ref[two, :])
            if half == 0:
                dk_ref[rows(b), :] = key_term
                dv_ref[rows(b), :] = value_term
            else:
                at = 2 * GROUP * HD + 2 * HD * b
                key_term = (dk_ref[rows(b), :] + key_term) * SCALE
                out_ref[:, pl.ds(at, HD)] = key_term.astype(bf16)
                out_ref[:, pl.ds(at + HD, HD)] = (dv_ref[rows(b), :] + value_term).astype(bf16)

    for step, g in (
        (score, 0), (score, 1), (weigh, 0), (score, 2), (weigh, 1), (attend, 0), (score, 3),
        (weigh, 2), (attend, 1), (back, 0), (weigh, 3), (attend, 2), (back, 1), (key_grads, 0),
        (attend, 3), (back, 2), (back, 3), (key_grads, 1),
    ):
        step(g)


VMEM = pl.BlockSpec(memory_space=pltpu.VMEM)
ANY = pl.BlockSpec(memory_space=pl.ANY)


def call(kernel, outs, scratch, *args, place_in=VMEM, place_out=VMEM, limit=LIMIT):
    return pl.pallas_call(
        kernel,
        out_shape=[jax.ShapeDtypeStruct(o, bf16) for o in outs],
        in_specs=[place_in] * len(args),
        out_specs=[place_out] * len(outs),
        scratch_shapes=scratch,
        compiler_params=pltpu.CompilerParams(vmem_limit_bytes=limit),
    )(*args)


def exchange(x, axes):
    return lax.all_to_all(x, axes, split_axis=0, concat_axis=0, tiled=True)


def per_device(queries, keys, values, grad_out, doc_lengths, positions):
    units, size = 256 * UNIT, UNIT * 32
    wide, narrow = (LOCAL, KVH * GROUP * HD), (LOCAL, KVH * HD)
    local = [pltpu.VMEM(s, bf16) for s in (wide, narrow, narrow, wide)]
    runs = jnp.pad(positions[::RUN] // RUN, (0, 4), constant_values=-1000)
    table = pl.pallas_call(
        table_kernel,
        out_shape=[
            jax.ShapeDtypeStruct(((BACK + 1) * BLOCK, BLOCK), bf16),
            jax.ShapeDtypeStruct((BLOCK, BLOCK), bf16),
            jax.ShapeDtypeStruct((size, size), bf16),
            jax.ShapeDtypeStruct((1, BLOCK), i32),
        ],
        in_specs=[VMEM, VMEM, pl.BlockSpec(memory_space=pltpu.SMEM)],
        out_specs=[VMEM] * 4,
        compiler_params=pltpu.CompilerParams(vmem_limit_bytes=LIMIT),
        cost_estimate=pl.CostEstimate(flops=1 << 24, bytes_accessed=1 << 18, transcendentals=0),
    )
    place_sort, place_unsort, place_unpack, begin = table(
        runs.reshape(1, 64), runs.reshape(64, 1), doc_lengths
    )
    (packed,) = call(
        pack_kernel,
        [(units, HD)],
        local
        + [
            pltpu.VMEM((size, KVH * HD), bf16),
            pltpu.VMEM((units, HD), bf16),
            pltpu.SemaphoreType.DMA((4,)),
            pltpu.SemaphoreType.DMA((4,)),
        ],
        queries,
        keys,
        values,
        grad_out,
        place_in=ANY,
        limit=None,
        place_out=ANY,
    )
    spread = exchange(packed.reshape(256, UNIT // 2, 2, HD), ALL).reshape(units, HD)
    (ordered,) = call(
        sort_kernel,
        [(BLOCK, 2048)],
        [pltpu.VMEM((units + 16, HD), f32), pltpu.VMEM((BLOCK, 1280), bf16)],
        spread,
        place_sort,
    )
    block = exchange(ordered.reshape(SPREAD, 8, 2048), SEQ_AXES).reshape(BLOCK, 2048)
    square = (GROUP * BLOCK, (BACK + 1) * BLOCK)
    (done,) = call(
        attention_kernel,
        [(BLOCK, 2048)],
        [
            pltpu.VMEM((square[1], BLOCK), f32),
            pltpu.VMEM(square, f32),
            pltpu.VMEM(square, f32),
            pltpu.VMEM(square, bf16),
            pltpu.VMEM(square, bf16),
        ]
        + [pltpu.VMEM((square[0], HD), bf16)] * 4
        + [pltpu.VMEM((square[1], HD), f32)] * 2,
        begin,
        block,
    )
    back = exchange(done.reshape(SPREAD, 8, 2048), SEQ_AXES)
    (unsorted,) = call(
        unsort_kernel,
        [(units, HD)],
        [
            pltpu.VMEM((units + 16, HD), f32),
            pltpu.VMEM((BLOCK, 256), f32),
            pltpu.VMEM((BLOCK, 1280), bf16),
        ],
        back,
        place_unsort,
    )
    home = exchange(unsorted.reshape(256, UNIT // 2, 2, HD), ALL).reshape(units, HD)
    return tuple(
        call(
            unpack_kernel,
            [wide, wide, narrow, narrow],
            local + [pltpu.VMEM((4, size, 2 * HD), bf16), pltpu.SemaphoreType.DMA((10,))],
            home,
            place_unpack,
            place_out=ANY,
        )
    )


def solution(mesh):
    parts = {"head": (("z_hi", 4), ("core", 2)), "inner": (("y", 4),), "outer": (("z_lo", 2), ("x", 4))}
    axes = [part for name in mesh.axis_names for part in parts[name]]
    split = Mesh(mesh.devices.reshape([size for _, size in axes]), [name for name, _ in axes])
    rows = P(ROWS, None)
    return jax.shard_map(
        per_device,
        mesh=split,
        in_specs=(rows, rows, rows, rows, P(), P()),
        out_specs=(rows, rows, rows, rows),
        check_vma=False,
    )
```

```python
import jax
import jax.numpy as jnp
from jax import lax
from jax.experimental import pallas as pl
from jax.experimental.pallas import tpu as pltpu
from jax.sharding import Mesh
from jax.sharding import PartitionSpec as P

HD = 128
GROUP = 4
KVH = 8
RUN = 128
BACK = 3
SPREAD = 32
BLOCK = 256
UNIT = 10
LOCAL = 30
SCALE = HD**-0.5
LOG2E = 1.4426950408889634
NEGATIVE = -1e30
ROWS = ("y", "z_lo", "x", "z_hi", "core")
ALL = ("z_hi", "z_lo", "y", "x", "core")
SEQ_AXES = ("y", "x", "core")
LIMIT = 48 * 1024 * 1024

f32, bf16, i32 = jnp.float32, jnp.bfloat16, jnp.int32


def iota(shape, dim):
    return lax.broadcasted_iota(i32, shape, dim)


def one_hot(condition):
    return jnp.where(condition, 1.0, 0.0).astype(bf16)


def dot(a, b):
    return jnp.dot(a, b, preferred_element_type=f32)


def dot_nt(a, b):
    return lax.dot_general(a, b, (((1,), (1,)), ((), ())), preferred_element_type=f32)


def first_row():
    device = 0
    for axis, size in zip(ROWS, (4, 2, 4, 4, 2)):
        device = device * size + lax.axis_index(axis)
    return (device * LOCAL) & (SPREAD - 1)


def seq_index():
    return lax.axis_index("y") * 8 + lax.axis_index("x") * 2 + lax.axis_index("core")


def spread_row(packed, shift):
    token = packed & 31
    to = ((shift + token) & 31) * UNIT + (packed >> 5)
    return jnp.where(token < LOCAL, to, -1)


def place_spread(rows_are_units):
    size = UNIT * 32
    to = spread_row(iota((size, size), int(rows_are_units)), first_row())
    return one_hot(iota((size, size), 1 - int(rows_are_units)) == to)


def pack_kernel(q_ref, k_ref, v_ref, g_ref, out_ref, qs, ks, vs, gs, x_ref, o_ref, in_sem, out_sem):
    size = UNIT * 32
    pairs = KVH // 2
    arrivals = []
    for i, (source, to) in enumerate(((q_ref, qs), (g_ref, gs), (k_ref, ks), (v_ref, vs))):
        arrivals.append(pltpu.make_async_copy(source, to, in_sem.at[i]))
        arrivals[-1].start()
    for u in range(UNIT):
        x_ref[pl.ds(u * 32 + 16, 16), :] = jnp.zeros((16, KVH * HD), bf16)
    place = place_spread(True)
    for copy in arrivals:
        copy.wait()
    departures = []
    for pair in range(pairs):
        for head in (2 * pair, 2 * pair + 1):
            to = pl.ds(head * HD, HD)
            for g in range(GROUP):
                column = pl.ds((head * GROUP + g) * HD, HD)
                x_ref[pl.ds(g * 32, LOCAL), to] = qs[:, column]
                x_ref[pl.ds((GROUP + g) * 32, LOCAL), to] = gs[:, column]
            x_ref[pl.ds(8 * 32, LOCAL), to] = ks[:, to]
            x_ref[pl.ds(9 * 32, LOCAL), to] = vs[:, to]
        rows = dot(place, x_ref[:, pl.ds(pair * 2 * HD, 2 * HD)]).astype(bf16)
        o_ref[pl.ds(2 * pair * size, size), :] = rows[:, :HD]
        o_ref[pl.ds((2 * pair + 1) * size, size), :] = rows[:, HD:]
        at = pl.ds(2 * pair * size, 2 * size)
        departures.append(pltpu.make_async_copy(o_ref.at[at, :], out_ref.at[at, :], out_sem.at[pair]))
        departures[-1].start()
    for copy in departures:
        copy.wait()


def unpack_kernel(r_ref, place_ref, att_ref, gq_ref, gk_ref, gv_ref, qs, ks, vs, gs, x_ref, sem):
    size = UNIT * 32
    pairs, half = KVH // 2, KVH * GROUP * HD // 2
    departures = []

    def send(source, to):
        departures.append(pltpu.make_async_copy(source, to, sem.at[len(departures)]))
        departures[-1].start()

    for pair in range(pairs):
        two = pl.ds(pair * 2 * HD, 2 * HD)
        for head in (2 * pair, 2 * pair + 1):
            x_ref[:, pl.ds(head * HD, HD)] = r_ref[pl.ds(head * size, size), :]
        rows = dot(place_ref[...], x_ref[:, two]).astype(bf16)
        for head in (2 * pair, 2 * pair + 1):
            part = rows[:, :HD] if head % 2 == 0 else rows[:, HD:]
            to = pl.ds(head * HD, HD)
            for g in range(GROUP):
                column = pl.ds((head * GROUP + g) * HD, HD)
                qs[:, column] = part[g * 32 : g * 32 + LOCAL]
                gs[:, column] = part[(GROUP + g) * 32 : (GROUP + g) * 32 + LOCAL]
            ks[:, to] = part[8 * 32 : 8 * 32 + LOCAL]
            vs[:, to] = part[9 * 32 : 9 * 32 + LOCAL]
        if pair % 2 == 1:
            at = pl.ds(pair // 2 * half, half)
            send(qs.at[:, at], att_ref.at[:, at])
            send(gs.at[:, at], gq_ref.at[:, at])
    send(ks, gk_ref)
    send(vs, gv_ref)
    for copy in departures:
        copy.wait()


def sender(run, slot, group):
    row = run * RUN + (slot & 3) * 32 + group
    device = (row * 34953) >> 20
    y, z_lo, x = device >> 6, (device >> 5) & 1, (device >> 3) & 3
    z_hi, core = (device >> 1) & 3, device & 1
    return jnp.where(run >= 0, z_hi * 64 + z_lo * 32 + y * 8 + x * 2 + core, -1)


def position(row):
    return ((row >> 2) & 1) * RUN + (row & 3) * 32 + (row >> 3)


def table_kernel(
    run_row_ref, run_col_ref, lengths_ref, sort_ref, unsort_ref, unpack_ref, begin_ref
):
    group = seq_index()
    query_pos = group * BLOCK + position(iota((1, BLOCK), 1))
    begin = jnp.zeros((1, BLOCK), i32)
    end = jnp.int32(0)
    for i in range(16):
        end = end + lengths_ref[i]
        begin = jnp.where(query_pos >= end, end, begin)
    begin_ref[...] = begin
    number = iota((BLOCK, 64), 1)
    for b in range(BACK + 1):
        slot = iota((BLOCK, 1), 0)
        found = run_row_ref[...] == (slot >> 2) - 2 * b
        run = jnp.max(jnp.where(found, number, -1), axis=1, keepdims=True)
        sort_ref[pl.ds(b * BLOCK, BLOCK), :] = one_hot(
            iota((BLOCK, BLOCK), 1) == sender(run, slot, group)
        )
    slot = iota((1, BLOCK), 1)
    found = run_col_ref[...] == (slot >> 2)
    run = jnp.max(jnp.where(found, iota((64, BLOCK), 0), -1), axis=0, keepdims=True)
    unsort_ref[...] = one_hot(iota((BLOCK, BLOCK), 0) == sender(run, slot, group))
    unpack_ref[...] = place_spread(False)


def sort_kernel(r_ref, place_ref, out_ref, wide_ref, x_ref):
    wide_ref[pl.ds(0, UNIT * BLOCK), :] = r_ref[...].astype(f32)
    for u in range(UNIT):
        x_ref[:, pl.ds(u * HD, HD)] = wide_ref[pl.ds(u, BLOCK, stride=UNIT), :].astype(bf16)
    out_ref[:, pl.ds(0, 1280)] = dot(place_ref[pl.ds(0, BLOCK), :], x_ref[...]).astype(bf16)
    for b in range(1, BACK + 1):
        out_ref[:, pl.ds(1024 + 256 * b, 256)] = dot(
            place_ref[pl.ds(b * BLOCK, BLOCK), :], x_ref[:, pl.ds(1024, 256)]
        ).astype(bf16)


def unsort_kernel(r_ref, place_ref, out_ref, wide_ref, sum_ref, x_ref):
    for b in range(BACK + 1):
        part = r_ref[b:SPREAD, :, pl.ds(1024 + 256 * b, 256)].astype(f32)
        part = part.reshape((SPREAD - b) * 8, 256)
        rows = pl.ds(0, (SPREAD - b) * 8)
        if b == 0:
            sum_ref[rows, :] = part
        else:
            sum_ref[rows, :] = sum_ref[rows, :] + part
    x_ref[:, pl.ds(0, 1024)] = r_ref[:, :, pl.ds(0, 1024)].reshape(BLOCK, 1024)
    x_ref[:, pl.ds(1024, 256)] = sum_ref[...].astype(bf16)
    for pair in range(UNIT // 2):
        rows = dot(place_ref[...], x_ref[:, pl.ds(pair * 2 * HD, 2 * HD)])
        wide_ref[pl.ds(2 * pair, BLOCK, stride=UNIT), :] = rows[:, :HD]
        wide_ref[pl.ds(2 * pair + 1, BLOCK, stride=UNIT), :] = rows[:, HD:]
    out_ref[...] = wide_ref[pl.ds(0, UNIT * BLOCK), :].astype(bf16)


def attention_kernel(
    begin_ref, m_ref, out_ref, bias_ref, s_ref, dp_ref, p_ref, d_ref, q_ref, g_ref, k_ref, v_ref,
    dk_ref, dv_ref,
):
    base = seq_index() * BLOCK
    blocks, heads = range(BACK + 1), range(GROUP)

    def rows(b):
        return pl.ds(b * BLOCK, BLOCK)

    query_pos = base + position(iota((1, BLOCK), 1))
    begin = begin_ref[...]
    key_pos = base + position(iota((BLOCK, BLOCK), 0))
    for b in blocks:
        seen = key_pos >= begin + b * BLOCK
        if b == 0:
            seen = seen & (key_pos <= query_pos)
        bias_ref[rows(b), :] = jnp.where(seen, 0.0, NEGATIVE)
        k_ref[rows(b), :] = m_ref[:, pl.ds(1024 + 256 * b, HD)]
        v_ref[rows(b), :] = m_ref[:, pl.ds(1024 + 256 * b + HD, HD)]
    for g in heads:
        q_ref[rows(g), :] = m_ref[:, pl.ds(g * HD, HD)]
        g_ref[rows(g), :] = m_ref[:, pl.ds((GROUP + g) * HD, HD)]
    keys, values = k_ref[...], v_ref[...]
    keys_t, values_t = keys.T, values.T

    tops, accums, inverses, deltas = {}, {}, {}, {}

    def score(g):
        s = dot_nt(keys, q_ref[rows(g), :]) * (SCALE * LOG2E) + bias_ref[...]
        s_ref[:, rows(g)] = s
        tops[g] = jnp.max(s, axis=0, keepdims=True)

    def weigh(g):
        weights = jnp.exp2(s_ref[:, rows(g)] - tops[g])
        s_ref[:, rows(g)] = weights
        inverses[g] = 1.0 / jnp.sum(weights, axis=0, keepdims=True)
        accums[g] = dot(values_t, weights.astype(bf16))
        dp_ref[:, rows(g)] = dot_nt(values, g_ref[rows(g), :])

    def attend(g):
        output = (accums[g] * inverses[g]).T.astype(bf16)
        out_ref[:, pl.ds(g * HD, HD)] = output
        product = g_ref[rows(g), :].astype(f32) * output.astype(f32)
        deltas[g] = jnp.sum(product.T, axis=0, keepdims=True)

    def back(g):
        prob = s_ref[:, rows(g)] * inverses[g]
        p_ref[:, rows(g)] = prob.astype(bf16)
        dscore = (prob * (dp_ref[:, rows(g)] - deltas[g])).astype(bf16)
        d_ref[:, rows(g)] = dscore
        out_ref[:, pl.ds((GROUP + g) * HD, HD)] = (dot(keys_t, dscore) * SCALE).T.astype(bf16)

    def key_grads(half):
        two = pl.ds(half * 2 * BLOCK, 2 * BLOCK)
        for b in blocks:
            key_term = dot(d_ref[rows(b), two], q_ref[two, :])
            value_term = dot(p_ref[rows(b), two], g_ref[two, :])
            if half == 0:
                dk_ref[rows(b), :] = key_term
                dv_ref[rows(b), :] = value_term
            else:
                at = 2 * GROUP * HD + 2 * HD * b
                key_term = (dk_ref[rows(b), :] + key_term) * SCALE
                out_ref[:, pl.ds(at, HD)] = key_term.astype(bf16)
                out_ref[:, pl.ds(at + HD, HD)] = (dv_ref[rows(b), :] + value_term).astype(bf16)

    for step, g in (
        (score, 0), (score, 1), (weigh, 0), (score, 2), (weigh, 1), (attend, 0), (score, 3),
        (weigh, 2), (attend, 1), (back, 0), (weigh, 3), (attend, 2), (back, 1), (key_grads, 0),
        (attend, 3), (back, 2), (back, 3), (key_grads, 1),
    ):
        step(g)


VMEM = pl.BlockSpec(memory_space=pltpu.VMEM)
ANY = pl.BlockSpec(memory_space=pl.ANY)


def call(kernel, outs, scratch, *args, place_in=VMEM, place_out=VMEM, limit=LIMIT):
    return pl.pallas_call(
        kernel,
        out_shape=[jax.ShapeDtypeStruct(o, bf16) for o in outs],
        in_specs=[place_in] * len(args),
        out_specs=[place_out] * len(outs),
        scratch_shapes=scratch,
        compiler_params=pltpu.CompilerParams(vmem_limit_bytes=limit),
    )(*args)


def exchange(x, axes):
    return lax.all_to_all(x, axes, split_axis=0, concat_axis=0, tiled=True)


def per_device(queries, keys, values, grad_out, doc_lengths, positions):
    units, size = 256 * UNIT, UNIT * 32
    wide, narrow = (LOCAL, KVH * GROUP * HD), (LOCAL, KVH * HD)
    local = [pltpu.VMEM(s, bf16) for s in (wide, narrow, narrow, wide)]
    runs = jnp.pad(positions[::RUN] // RUN, (0, 4), constant_values=-1000)
    table = pl.pallas_call(
        table_kernel,
        out_shape=[
            jax.ShapeDtypeStruct(((BACK + 1) * BLOCK, BLOCK), bf16),
            jax.ShapeDtypeStruct((BLOCK, BLOCK), bf16),
            jax.ShapeDtypeStruct((size, size), bf16),
            jax.ShapeDtypeStruct((1, BLOCK), i32),
        ],
        in_specs=[VMEM, VMEM, pl.BlockSpec(memory_space=pltpu.SMEM)],
        out_specs=[VMEM] * 4,
        compiler_params=pltpu.CompilerParams(vmem_limit_bytes=LIMIT),
        cost_estimate=pl.CostEstimate(flops=1 << 24, bytes_accessed=1 << 18, transcendentals=0),
    )
    place_sort, place_unsort, place_unpack, begin = table(
        runs.reshape(1, 64), runs.reshape(64, 1), doc_lengths
    )
    (packed,) = call(
        pack_kernel,
        [(units, HD)],
        local
        + [
            pltpu.VMEM((size, KVH * HD), bf16),
            pltpu.VMEM((units, HD), bf16),
            pltpu.SemaphoreType.DMA((4,)),
            pltpu.SemaphoreType.DMA((4,)),
        ],
        queries,
        keys,
        values,
        grad_out,
        place_in=ANY,
        limit=None,
        place_out=ANY,
    )
    spread = exchange(packed.reshape(256, UNIT // 2, 2, HD), ALL).reshape(units, HD)
    (ordered,) = call(
        sort_kernel,
        [(BLOCK, 2048)],
        [pltpu.VMEM((units + 16, HD), f32), pltpu.VMEM((BLOCK, 1280), bf16)],
        spread,
        place_sort,
    )
    block = exchange(ordered.reshape(SPREAD, 8, 2048), SEQ_AXES).reshape(BLOCK, 2048)
    square = (GROUP * BLOCK, (BACK + 1) * BLOCK)
    (done,) = call(
        attention_kernel,
        [(BLOCK, 2048)],
        [
            pltpu.VMEM((square[1], BLOCK), f32),
            pltpu.VMEM(square, f32),
            pltpu.VMEM(square, f32),
            pltpu.VMEM(square, bf16),
            pltpu.VMEM(square, bf16),
        ]
        + [pltpu.VMEM((square[0], HD), bf16)] * 4
        + [pltpu.VMEM((square[1], HD), f32)] * 2,
        begin,
        block,
    )
    back = exchange(done.reshape(SPREAD, 8, 2048), SEQ_AXES)
    (unsorted,) = call(
        unsort_kernel,
        [(units, HD)],
        [
            pltpu.VMEM((units + 16, HD), f32),
            pltpu.VMEM((BLOCK, 256), f32),
            pltpu.VMEM((BLOCK, 1280), bf16),
        ],
        back,
        place_unsort,
    )
    home = exchange(unsorted.reshape(256, UNIT // 2, 2, HD), ALL).reshape(units, HD)
    return tuple(
        call(
            unpack_kernel,
            [wide, wide, narrow, narrow],
            local + [pltpu.VMEM((size, KVH * HD), bf16), pltpu.SemaphoreType.DMA((6,))],
            home,
            place_unpack,
            place_out=ANY,
        )
    )


def solution(mesh):
    parts = {"head": (("z_hi", 4), ("core", 2)), "inner": (("y", 4),), "outer": (("z_lo", 2), ("x", 4))}
    axes = [part for name in mesh.axis_names for part in parts[name]]
    split = Mesh(mesh.devices.reshape([size for _, size in axes]), [name for name, _ in axes])
    rows = P(ROWS, None)
    return jax.shard_map(
        per_device,
        mesh=split,
        in_specs=(rows, rows, rows, rows, P(), P()),
        out_specs=(rows, rows, rows, rows),
        check_vma=False,
    )
```

```python
import jax
import jax.numpy as jnp
from jax import lax
from jax.experimental import pallas as pl
from jax.experimental.pallas import tpu as pltpu
from jax.sharding import Mesh
from jax.sharding import PartitionSpec as P

HD = 128
GROUP = 4
KVH = 8
RUN = 128
BACK = 3
SPREAD = 32
BLOCK = 256
UNIT = 10
LOCAL = 30
SCALE = HD**-0.5
LOG2E = 1.4426950408889634
NEGATIVE = -1e30
ROWS = ("y", "z_lo", "x", "z_hi", "core")
ALL = ("z_hi", "z_lo", "y", "x", "core")
SEQ_AXES = ("y", "x", "core")
LIMIT = 48 * 1024 * 1024

f32, bf16, i32 = jnp.float32, jnp.bfloat16, jnp.int32


def iota(shape, dim):
    return lax.broadcasted_iota(i32, shape, dim)


def one_hot(condition):
    return jnp.where(condition, 1.0, 0.0).astype(bf16)


def dot(a, b):
    return jnp.dot(a, b, preferred_element_type=f32)


def dot_nt(a, b):
    return lax.dot_general(a, b, (((1,), (1,)), ((), ())), preferred_element_type=f32)


def first_row():
    device = 0
    for axis, size in zip(ROWS, (4, 2, 4, 4, 2)):
        device = device * size + lax.axis_index(axis)
    return (device * LOCAL) & (SPREAD - 1)


def seq_index():
    return lax.axis_index("y") * 8 + lax.axis_index("x") * 2 + lax.axis_index("core")


def spread_row(packed, shift):
    token = packed & 31
    to = ((shift + token) & 31) * UNIT + (packed >> 5)
    return jnp.where(token < LOCAL, to, -1)


def place_spread(rows_are_units):
    size = UNIT * 32
    to = spread_row(iota((size, size), int(rows_are_units)), first_row())
    return one_hot(iota((size, size), 1 - int(rows_are_units)) == to)


def pack_kernel(q_ref, k_ref, v_ref, g_ref, out_ref, qs, ks, vs, gs, x_ref, o_ref, in_sem, out_sem):
    size = UNIT * 32
    pairs = KVH // 2
    arrivals = []
    for i, (source, to) in enumerate(((q_ref, qs), (g_ref, gs), (k_ref, ks), (v_ref, vs))):
        arrivals.append(pltpu.make_async_copy(source, to, in_sem.at[i]))
        arrivals[-1].start()
    for u in range(UNIT):
        x_ref[pl.ds(u * 32 + 16, 16), :] = jnp.zeros((16, KVH * HD), bf16)
    place = place_spread(True)
    for copy in arrivals:
        copy.wait()
    departures = []
    for pair in range(pairs):
        for head in (2 * pair, 2 * pair + 1):
            to = pl.ds(head * HD, HD)
            for g in range(GROUP):
                column = pl.ds((head * GROUP + g) * HD, HD)
                x_ref[pl.ds(g * 32, LOCAL), to] = qs[:, column]
                x_ref[pl.ds((GROUP + g) * 32, LOCAL), to] = gs[:, column]
            x_ref[pl.ds(8 * 32, LOCAL), to] = ks[:, to]
            x_ref[pl.ds(9 * 32, LOCAL), to] = vs[:, to]
        rows = dot(place, x_ref[:, pl.ds(pair * 2 * HD, 2 * HD)]).astype(bf16)
        o_ref[pl.ds(2 * pair * size, size), :] = rows[:, :HD]
        o_ref[pl.ds((2 * pair + 1) * size, size), :] = rows[:, HD:]
        at = pl.ds(2 * pair * size, 2 * size)
        departures.append(pltpu.make_async_copy(o_ref.at[at, :], out_ref.at[at, :], out_sem.at[pair]))
        departures[-1].start()
    for copy in departures:
        copy.wait()


def unpack_kernel(r_ref, place_ref, att_ref, gq_ref, gk_ref, gv_ref, qs, ks, vs, gs, x_ref, sem):
    size = UNIT * 32
    pairs, half = KVH // 2, KVH * GROUP * HD // 2
    departures = []

    def send(source, to):
        departures.append(pltpu.make_async_copy(source, to, sem.at[len(departures)]))
        departures[-1].start()

    for pair in range(pairs):
        two = pl.ds(pair * 2 * HD, 2 * HD)
        for head in (2 * pair, 2 * pair + 1):
            x_ref[:, pl.ds(head * HD, HD)] = r_ref[pl.ds(head * size, size), :]
        rows = dot(place_ref[...], x_ref[:, two]).astype(bf16)
        for head in (2 * pair, 2 * pair + 1):
            part = rows[:, :HD] if head % 2 == 0 else rows[:, HD:]
            to = pl.ds(head * HD, HD)
            for g in range(GROUP):
                column = pl.ds((head * GROUP + g) * HD, HD)
                qs[:, column] = part[g * 32 : g * 32 + LOCAL]
                gs[:, column] = part[(GROUP + g) * 32 : (GROUP + g) * 32 + LOCAL]
            ks[:, to] = part[8 * 32 : 8 * 32 + LOCAL]
            vs[:, to] = part[9 * 32 : 9 * 32 + LOCAL]
        if pair % 2 == 1:
            at = pl.ds(pair // 2 * half, half)
            send(qs.at[:, at], att_ref.at[:, at])
            send(gs.at[:, at], gq_ref.at[:, at])
    send(ks, gk_ref)
    send(vs, gv_ref)
    for copy in departures:
        copy.wait()


def sender(run, slot, group):
    row = run * RUN + (slot & 3) * 32 + group
    device = (row * 34953) >> 20
    y, z_lo, x = device >> 6, (device >> 5) & 1, (device >> 3) & 3
    z_hi, core = (device >> 1) & 3, device & 1
    return jnp.where(run >= 0, z_hi * 64 + z_lo * 32 + y * 8 + x * 2 + core, -1)


def position(row):
    return ((row >> 2) & 1) * RUN + (row & 3) * 32 + (row >> 3)


def table_kernel(
    run_row_ref, run_col_ref, lengths_ref, sort_ref, unsort_ref, unpack_ref, begin_ref
):
    group = seq_index()
    query_pos = group * BLOCK + position(iota((1, BLOCK), 1))
    begin = jnp.zeros((1, BLOCK), i32)
    end = jnp.int32(0)
    for i in range(16):
        end = end + lengths_ref[i]
        begin = jnp.where(query_pos >= end, end, begin)
    begin_ref[...] = begin
    number = iota((BLOCK, 64), 1)
    for b in range(BACK + 1):
        slot = iota((BLOCK, 1), 0)
        found = run_row_ref[...] == (slot >> 2) - 2 * b
        run = jnp.max(jnp.where(found, number, -1), axis=1, keepdims=True)
        sort_ref[pl.ds(b * BLOCK, BLOCK), :] = one_hot(
            iota((BLOCK, BLOCK), 1) == sender(run, slot, group)
        )
    slot = iota((1, BLOCK), 1)
    found = run_col_ref[...] == (slot >> 2)
    run = jnp.max(jnp.where(found, iota((64, BLOCK), 0), -1), axis=0, keepdims=True)
    unsort_ref[...] = one_hot(iota((BLOCK, BLOCK), 0) == sender(run, slot, group))
    unpack_ref[...] = place_spread(False)


def sort_kernel(r_ref, place_ref, out_ref, wide_ref, x_ref):
    wide_ref[pl.ds(0, UNIT * BLOCK), :] = r_ref[...].astype(f32)
    for u in range(UNIT):
        x_ref[:, pl.ds(u * HD, HD)] = wide_ref[pl.ds(u, BLOCK, stride=UNIT), :].astype(bf16)
    out_ref[:, pl.ds(0, 1280)] = dot(place_ref[pl.ds(0, BLOCK), :], x_ref[...]).astype(bf16)
    for b in range(1, BACK + 1):
        out_ref[:, pl.ds(1024 + 256 * b, 256)] = dot(
            place_ref[pl.ds(b * BLOCK, BLOCK), :], x_ref[:, pl.ds(1024, 256)]
        ).astype(bf16)


def unsort_kernel(r_ref, place_ref, out_ref, wide_ref, sum_ref, x_ref):
    for b in range(BACK + 1):
        part = r_ref[b:SPREAD, :, pl.ds(1024 + 256 * b, 256)].astype(f32)
        part = part.reshape((SPREAD - b) * 8, 256)
        rows = pl.ds(0, (SPREAD - b) * 8)
        if b == 0:
            sum_ref[rows, :] = part
        else:
            sum_ref[rows, :] = sum_ref[rows, :] + part
    x_ref[:, pl.ds(0, 1024)] = r_ref[:, :, pl.ds(0, 1024)].reshape(BLOCK, 1024)
    x_ref[:, pl.ds(1024, 256)] = sum_ref[...].astype(bf16)
    for pair in range(UNIT // 2):
        rows = dot(place_ref[...], x_ref[:, pl.ds(pair * 2 * HD, 2 * HD)])
        wide_ref[pl.ds(2 * pair, BLOCK, stride=UNIT), :] = rows[:, :HD]
        wide_ref[pl.ds(2 * pair + 1, BLOCK, stride=UNIT), :] = rows[:, HD:]
    out_ref[...] = wide_ref[pl.ds(0, UNIT * BLOCK), :].astype(bf16)


def attention_kernel(
    begin_ref, m_ref, out_ref, bias_ref, s_ref, dp_ref, p_ref, d_ref, dk_ref, dv_ref,
):
    base = seq_index() * BLOCK
    blocks, heads = range(BACK + 1), range(GROUP)

    def rows(b):
        return pl.ds(b * BLOCK, BLOCK)

    query_pos = base + position(iota((1, BLOCK), 1))
    begin = begin_ref[...]
    key_pos = base + position(iota((BLOCK, BLOCK), 0))
    for b in blocks:
        seen = key_pos >= begin + b * BLOCK
        if b == 0:
            seen = seen & (key_pos <= query_pos)
        bias_ref[rows(b), :] = jnp.where(seen, 0.0, NEGATIVE)

    def joined(first, count, step=HD):
        parts = [m_ref[:, pl.ds(first + step * i, HD)] for i in range(count)]
        return jnp.concatenate(parts, axis=0)

    keys, values = joined(2 * GROUP * HD, BACK + 1, 2 * HD), joined(2 * GROUP * HD + HD, BACK + 1, 2 * HD)
    queries = [m_ref[:, pl.ds(g * HD, HD)] for g in heads]
    grads = [m_ref[:, pl.ds((GROUP + g) * HD, HD)] for g in heads]
    keys_t, values_t = keys.T, values.T

    tops, accums, inverses, deltas = {}, {}, {}, {}

    def score(g):
        s = dot_nt(keys, queries[g]) * (SCALE * LOG2E) + bias_ref[...]
        s_ref[:, rows(g)] = s
        tops[g] = jnp.max(s, axis=0, keepdims=True)

    def weigh(g):
        weights = jnp.exp2(s_ref[:, rows(g)] - tops[g])
        s_ref[:, rows(g)] = weights
        inverses[g] = 1.0 / jnp.sum(weights, axis=0, keepdims=True)
        accums[g] = dot(values_t, weights.astype(bf16))
        dp_ref[:, rows(g)] = dot_nt(values, grads[g])

    def attend(g):
        output = (accums[g] * inverses[g]).T.astype(bf16)
        out_ref[:, pl.ds(g * HD, HD)] = output
        product = grads[g].astype(f32) * output.astype(f32)
        deltas[g] = jnp.sum(product.T, axis=0, keepdims=True)

    def back(g):
        prob = s_ref[:, rows(g)] * inverses[g]
        p_ref[:, rows(g)] = prob.astype(bf16)
        dscore = (prob * (dp_ref[:, rows(g)] - deltas[g])).astype(bf16)
        d_ref[:, rows(g)] = dscore
        out_ref[:, pl.ds((GROUP + g) * HD, HD)] = (dot(keys_t, dscore) * SCALE).T.astype(bf16)

    def key_grads(half):
        two = pl.ds(half * 2 * BLOCK, 2 * BLOCK)
        query, grad = joined(half * 2 * HD, 2), joined((GROUP + 2 * half) * HD, 2)
        for b in blocks:
            key_term = dot(d_ref[rows(b), two], query)
            value_term = dot(p_ref[rows(b), two], grad)
            if half == 0:
                dk_ref[rows(b), :] = key_term
                dv_ref[rows(b), :] = value_term
            else:
                at = 2 * GROUP * HD + 2 * HD * b
                key_term = (dk_ref[rows(b), :] + key_term) * SCALE
                out_ref[:, pl.ds(at, HD)] = key_term.astype(bf16)
                out_ref[:, pl.ds(at + HD, HD)] = (dv_ref[rows(b), :] + value_term).astype(bf16)

    for step, g in (
        (score, 0), (score, 1), (weigh, 0), (score, 2), (weigh, 1), (attend, 0), (score, 3),
        (weigh, 2), (attend, 1), (back, 0), (weigh, 3), (attend, 2), (back, 1), (key_grads, 0),
        (attend, 3), (back, 2), (back, 3), (key_grads, 1),
    ):
        step(g)


VMEM = pl.BlockSpec(memory_space=pltpu.VMEM)
ANY = pl.BlockSpec(memory_space=pl.ANY)


def call(kernel, outs, scratch, *args, place_in=VMEM, place_out=VMEM, limit=LIMIT):
    return pl.pallas_call(
        kernel,
        out_shape=[jax.ShapeDtypeStruct(o, bf16) for o in outs],
        in_specs=[place_in] * len(args),
        out_specs=[place_out] * len(outs),
        scratch_shapes=scratch,
        compiler_params=pltpu.CompilerParams(vmem_limit_bytes=limit),
    )(*args)


def exchange(x, axes):
    return lax.all_to_all(x, axes, split_axis=0, concat_axis=0, tiled=True)


def per_device(queries, keys, values, grad_out, doc_lengths, positions):
    units, size = 256 * UNIT, UNIT * 32
    wide, narrow = (LOCAL, KVH * GROUP * HD), (LOCAL, KVH * HD)
    local = [pltpu.VMEM(s, bf16) for s in (wide, narrow, narrow, wide)]
    runs = jnp.pad(positions[::RUN] // RUN, (0, 4), constant_values=-1000)
    table = pl.pallas_call(
        table_kernel,
        out_shape=[
            jax.ShapeDtypeStruct(((BACK + 1) * BLOCK, BLOCK), bf16),
            jax.ShapeDtypeStruct((BLOCK, BLOCK), bf16),
            jax.ShapeDtypeStruct((size, size), bf16),
            jax.ShapeDtypeStruct((1, BLOCK), i32),
        ],
        in_specs=[VMEM, VMEM, pl.BlockSpec(memory_space=pltpu.SMEM)],
        out_specs=[VMEM] * 4,
        compiler_params=pltpu.CompilerParams(vmem_limit_bytes=LIMIT),
        cost_estimate=pl.CostEstimate(flops=1 << 24, bytes_accessed=1 << 18, transcendentals=0),
    )
    place_sort, place_unsort, place_unpack, begin = table(
        runs.reshape(1, 64), runs.reshape(64, 1), doc_lengths
    )
    (packed,) = call(
        pack_kernel,
        [(units, HD)],
        local
        + [
            pltpu.VMEM((size, KVH * HD), bf16),
            pltpu.VMEM((units, HD), bf16),
            pltpu.SemaphoreType.DMA((4,)),
            pltpu.SemaphoreType.DMA((4,)),
        ],
        queries,
        keys,
        values,
        grad_out,
        place_in=ANY,
        limit=None,
        place_out=ANY,
    )
    spread = exchange(packed.reshape(256, UNIT // 2, 2, HD), ALL).reshape(units, HD)
    (ordered,) = call(
        sort_kernel,
        [(BLOCK, 2048)],
        [pltpu.VMEM((units + 16, HD), f32), pltpu.VMEM((BLOCK, 1280), bf16)],
        spread,
        place_sort,
    )
    block = exchange(ordered.reshape(SPREAD, 8, 2048), SEQ_AXES).reshape(BLOCK, 2048)
    square = (GROUP * BLOCK, (BACK + 1) * BLOCK)
    (done,) = call(
        attention_kernel,
        [(BLOCK, 2048)],
        [
            pltpu.VMEM((square[1], BLOCK), f32),
            pltpu.VMEM(square, f32),
            pltpu.VMEM(square, f32),
            pltpu.VMEM(square, bf16),
            pltpu.VMEM(square, bf16),
        ]
        + [pltpu.VMEM((square[1], HD), f32)] * 2,
        begin,
        block,
    )
    back = exchange(done.reshape(SPREAD, 8, 2048), SEQ_AXES)
    (unsorted,) = call(
        unsort_kernel,
        [(units, HD)],
        [
            pltpu.VMEM((units + 16, HD), f32),
            pltpu.VMEM((BLOCK, 256), f32),
            pltpu.VMEM((BLOCK, 1280), bf16),
        ],
        back,
        place_unsort,
    )
    home = exchange(unsorted.reshape(256, UNIT // 2, 2, HD), ALL).reshape(units, HD)
    return tuple(
        call(
            unpack_kernel,
            [wide, wide, narrow, narrow],
            local + [pltpu.VMEM((size, KVH * HD), bf16), pltpu.SemaphoreType.DMA((6,))],
            home,
            place_unpack,
            place_out=ANY,
        )
    )


def solution(mesh):
    parts = {"head": (("z_hi", 4), ("core", 2)), "inner": (("y", 4),), "outer": (("z_lo", 2), ("x", 4))}
    axes = [part for name in mesh.axis_names for part in parts[name]]
    split = Mesh(mesh.devices.reshape([size for _, size in axes]), [name for name, _ in axes])
    rows = P(ROWS, None)
    return jax.shard_map(
        per_device,
        mesh=split,
        in_specs=(rows, rows, rows, rows, P(), P()),
        out_specs=(rows, rows, rows, rows),
        check_vma=False,
    )
```

```python
import jax
import jax.numpy as jnp
from jax import lax
from jax.experimental import pallas as pl
from jax.experimental.pallas import tpu as pltpu
from jax.sharding import Mesh
from jax.sharding import PartitionSpec as P

HD = 128
GROUP = 4
KVH = 8
RUN = 128
BACK = 3
SPREAD = 32
BLOCK = 256
UNIT = 10
LOCAL = 30
SCALE = HD**-0.5
LOG2E = 1.4426950408889634
NEGATIVE = -1e30
ROWS = ("y", "z_lo", "x", "z_hi", "core")
ALL = ("z_hi", "z_lo", "y", "x", "core")
SEQ_AXES = ("y", "x", "core")
LIMIT = 48 * 1024 * 1024

f32, bf16, i32 = jnp.float32, jnp.bfloat16, jnp.int32


def iota(shape, dim):
    return lax.broadcasted_iota(i32, shape, dim)


def one_hot(condition):
    return jnp.where(condition, 1.0, 0.0).astype(bf16)


def dot(a, b):
    return jnp.dot(a, b, preferred_element_type=f32)


def dot_nt(a, b):
    return lax.dot_general(a, b, (((1,), (1,)), ((), ())), preferred_element_type=f32)


def first_row():
    device = 0
    for axis, size in zip(ROWS, (4, 2, 4, 4, 2)):
        device = device * size + lax.axis_index(axis)
    return (device * LOCAL) & (SPREAD - 1)


def seq_index():
    return lax.axis_index("y") * 8 + lax.axis_index("x") * 2 + lax.axis_index("core")


def spread_row(packed, shift):
    token = packed & 31
    to = ((shift + token) & 31) * UNIT + (packed >> 5)
    return jnp.where(token < LOCAL, to, -1)


def place_spread(rows_are_units):
    size = UNIT * 32
    to = spread_row(iota((size, size), int(rows_are_units)), first_row())
    return one_hot(iota((size, size), 1 - int(rows_are_units)) == to)


def pack_kernel(q_ref, k_ref, v_ref, g_ref, out_ref, qs, ks, vs, gs, x_ref, o_ref, in_sem, out_sem):
    size = UNIT * 32
    pairs = KVH // 2
    arrivals = []
    for i, (source, to) in enumerate(((q_ref, qs), (g_ref, gs), (k_ref, ks), (v_ref, vs))):
        arrivals.append(pltpu.make_async_copy(source, to, in_sem.at[i]))
        arrivals[-1].start()
    for u in range(UNIT):
        x_ref[pl.ds(u * 32 + 16, 16), :] = jnp.zeros((16, KVH * HD), bf16)
    place = place_spread(True)
    for copy in arrivals:
        copy.wait()
    departures = []
    for pair in range(pairs):
        for head in (2 * pair, 2 * pair + 1):
            to = pl.ds(head * HD, HD)
            for g in range(GROUP):
                column = pl.ds((head * GROUP + g) * HD, HD)
                x_ref[pl.ds(g * 32, LOCAL), to] = qs[:, column]
                x_ref[pl.ds((GROUP + g) * 32, LOCAL), to] = gs[:, column]
            x_ref[pl.ds(8 * 32, LOCAL), to] = ks[:, to]
            x_ref[pl.ds(9 * 32, LOCAL), to] = vs[:, to]
        rows = dot(place, x_ref[:, pl.ds(pair * 2 * HD, 2 * HD)]).astype(bf16)
        o_ref[pl.ds(2 * pair * size, size), :] = rows[:, :HD]
        o_ref[pl.ds((2 * pair + 1) * size, size), :] = rows[:, HD:]
        at = pl.ds(2 * pair * size, 2 * size)
        departures.append(pltpu.make_async_copy(o_ref.at[at, :], out_ref.at[at, :], out_sem.at[pair]))
        departures[-1].start()
    for copy in departures:
        copy.wait()


def unpack_kernel(r_ref, place_ref, att_ref, gq_ref, gk_ref, gv_ref, qs, ks, vs, gs, sem):
    size = UNIT * 32
    pairs, half = KVH // 2, KVH * GROUP * HD // 2
    departures = []

    def send(source, to):
        departures.append(pltpu.make_async_copy(source, to, sem.at[len(departures)]))
        departures[-1].start()

    for pair in range(pairs):
        units = [r_ref[pl.ds((2 * pair + i) * size, size), :] for i in range(2)]
        rows = dot(place_ref[...], jnp.concatenate(units, axis=1)).astype(bf16)
        for head in (2 * pair, 2 * pair + 1):
            part = rows[:, :HD] if head % 2 == 0 else rows[:, HD:]
            to = pl.ds(head * HD, HD)
            for g in range(GROUP):
                column = pl.ds((head * GROUP + g) * HD, HD)
                qs[:, column] = part[g * 32 : g * 32 + LOCAL]
                gs[:, column] = part[(GROUP + g) * 32 : (GROUP + g) * 32 + LOCAL]
            ks[:, to] = part[8 * 32 : 8 * 32 + LOCAL]
            vs[:, to] = part[9 * 32 : 9 * 32 + LOCAL]
        if pair % 2 == 1:
            at = pl.ds(pair // 2 * half, half)
            send(qs.at[:, at], att_ref.at[:, at])
            send(gs.at[:, at], gq_ref.at[:, at])
    send(ks, gk_ref)
    send(vs, gv_ref)
    for copy in departures:
        copy.wait()


def sender(run, slot, group):
    row = run * RUN + (slot & 3) * 32 + group
    device = (row * 34953) >> 20
    y, z_lo, x = device >> 6, (device >> 5) & 1, (device >> 3) & 3
    z_hi, core = (device >> 1) & 3, device & 1
    return jnp.where(run >= 0, z_hi * 64 + z_lo * 32 + y * 8 + x * 2 + core, -1)


def position(row):
    return ((row >> 2) & 1) * RUN + (row & 3) * 32 + (row >> 3)


def table_kernel(
    run_row_ref, run_col_ref, lengths_ref, sort_ref, unsort_ref, unpack_ref, begin_ref
):
    group = seq_index()
    query_pos = group * BLOCK + position(iota((1, BLOCK), 1))
    begin = jnp.zeros((1, BLOCK), i32)
    end = jnp.int32(0)
    for i in range(16):
        end = end + lengths_ref[i]
        begin = jnp.where(query_pos >= end, end, begin)
    begin_ref[...] = begin
    number = iota((BLOCK, 64), 1)
    for b in range(BACK + 1):
        slot = iota((BLOCK, 1), 0)
        found = run_row_ref[...] == (slot >> 2) - 2 * b
        run = jnp.max(jnp.where(found, number, -1), axis=1, keepdims=True)
        sort_ref[pl.ds(b * BLOCK, BLOCK), :] = one_hot(
            iota((BLOCK, BLOCK), 1) == sender(run, slot, group)
        )
    slot = iota((1, BLOCK), 1)
    found = run_col_ref[...] == (slot >> 2)
    run = jnp.max(jnp.where(found, iota((64, BLOCK), 0), -1), axis=0, keepdims=True)
    unsort_ref[...] = one_hot(iota((BLOCK, BLOCK), 0) == sender(run, slot, group))
    unpack_ref[...] = place_spread(False)


def sort_kernel(r_ref, place_ref, out_ref, wide_ref):
    wide_ref[pl.ds(0, UNIT * BLOCK), :] = r_ref[...].astype(f32)
    units = [wide_ref[pl.ds(u, BLOCK, stride=UNIT), :].astype(bf16) for u in range(UNIT)]
    pairs = [jnp.concatenate(units[u : u + 2], axis=1) for u in range(0, UNIT, 2)]
    for i, pair in enumerate(pairs):
        rows = dot(place_ref[pl.ds(0, BLOCK), :], pair)
        out_ref[:, pl.ds(2 * HD * i, 2 * HD)] = rows.astype(bf16)
    for b in range(1, BACK + 1):
        out_ref[:, pl.ds(1024 + 256 * b, 256)] = dot(
            place_ref[pl.ds(b * BLOCK, BLOCK), :], pairs[-1]
        ).astype(bf16)


def unsort_kernel(r_ref, place_ref, out_ref, wide_ref, sum_ref, x_ref):
    for b in range(BACK + 1):
        part = r_ref[b:SPREAD, :, pl.ds(1024 + 256 * b, 256)].astype(f32)
        part = part.reshape((SPREAD - b) * 8, 256)
        rows = pl.ds(0, (SPREAD - b) * 8)
        if b == 0:
            sum_ref[rows, :] = part
        else:
            sum_ref[rows, :] = sum_ref[rows, :] + part
    x_ref[:, pl.ds(0, 1024)] = r_ref[:, :, pl.ds(0, 1024)].reshape(BLOCK, 1024)
    x_ref[:, pl.ds(1024, 256)] = sum_ref[...].astype(bf16)
    for pair in range(UNIT // 2):
        rows = dot(place_ref[...], x_ref[:, pl.ds(pair * 2 * HD, 2 * HD)])
        wide_ref[pl.ds(2 * pair, BLOCK, stride=UNIT), :] = rows[:, :HD]
        wide_ref[pl.ds(2 * pair + 1, BLOCK, stride=UNIT), :] = rows[:, HD:]
    out_ref[...] = wide_ref[pl.ds(0, UNIT * BLOCK), :].astype(bf16)


def attention_kernel(
    begin_ref, m_ref, out_ref, bias_ref, s_ref, dp_ref, p_ref, d_ref, dk_ref, dv_ref,
):
    base = seq_index() * BLOCK
    blocks, heads = range(BACK + 1), range(GROUP)

    def rows(b):
        return pl.ds(b * BLOCK, BLOCK)

    query_pos = base + position(iota((1, BLOCK), 1))
    begin = begin_ref[...]
    key_pos = base + position(iota((BLOCK, BLOCK), 0))
    for b in blocks:
        seen = key_pos >= begin + b * BLOCK
        if b == 0:
            seen = seen & (key_pos <= query_pos)
        bias_ref[rows(b), :] = jnp.where(seen, 0.0, NEGATIVE)

    def joined(first, count, step=HD):
        parts = [m_ref[:, pl.ds(first + step * i, HD)] for i in range(count)]
        return jnp.concatenate(parts, axis=0)

    keys, values = joined(2 * GROUP * HD, BACK + 1, 2 * HD), joined(2 * GROUP * HD + HD, BACK + 1, 2 * HD)
    queries = [m_ref[:, pl.ds(g * HD, HD)] for g in heads]
    grads = [m_ref[:, pl.ds((GROUP + g) * HD, HD)] for g in heads]
    keys_t, values_t = keys.T, values.T

    tops, accums, inverses, deltas = {}, {}, {}, {}

    def score(g):
        s = dot_nt(keys, queries[g]) * (SCALE * LOG2E) + bias_ref[...]
        s_ref[:, rows(g)] = s
        tops[g] = jnp.max(s, axis=0, keepdims=True)

    def weigh(g):
        weights = jnp.exp2(s_ref[:, rows(g)] - tops[g])
        s_ref[:, rows(g)] = weights
        inverses[g] = 1.0 / jnp.sum(weights, axis=0, keepdims=True)
        accums[g] = dot(values_t, weights.astype(bf16))
        dp_ref[:, rows(g)] = dot_nt(values, grads[g])

    def attend(g):
        output = (accums[g] * inverses[g]).T.astype(bf16)
        out_ref[:, pl.ds(g * HD, HD)] = output
        product = grads[g].astype(f32) * output.astype(f32)
        deltas[g] = jnp.sum(product.T, axis=0, keepdims=True)

    def back(g):
        prob = s_ref[:, rows(g)] * inverses[g]
        p_ref[:, rows(g)] = prob.astype(bf16)
        dscore = (prob * (dp_ref[:, rows(g)] - deltas[g])).astype(bf16)
        d_ref[:, rows(g)] = dscore
        out_ref[:, pl.ds((GROUP + g) * HD, HD)] = (dot(keys_t, dscore) * SCALE).T.astype(bf16)

    def key_grads(half):
        two = pl.ds(half * 2 * BLOCK, 2 * BLOCK)
        query, grad = joined(half * 2 * HD, 2), joined((GROUP + 2 * half) * HD, 2)
        for b in blocks:
            key_term = dot(d_ref[rows(b), two], query)
            value_term = dot(p_ref[rows(b), two], grad)
            if half == 0:
                dk_ref[rows(b), :] = key_term
                dv_ref[rows(b), :] = value_term
            else:
                at = 2 * GROUP * HD + 2 * HD * b
                key_term = (dk_ref[rows(b), :] + key_term) * SCALE
                out_ref[:, pl.ds(at, HD)] = key_term.astype(bf16)
                out_ref[:, pl.ds(at + HD, HD)] = (dv_ref[rows(b), :] + value_term).astype(bf16)

    for step, g in (
        (score, 0), (score, 1), (weigh, 0), (score, 2), (weigh, 1), (attend, 0), (score, 3),
        (weigh, 2), (attend, 1), (back, 0), (weigh, 3), (attend, 2), (back, 1), (key_grads, 0),
        (attend, 3), (back, 2), (back, 3), (key_grads, 1),
    ):
        step(g)


VMEM = pl.BlockSpec(memory_space=pltpu.VMEM)
ANY = pl.BlockSpec(memory_space=pl.ANY)


def call(kernel, outs, scratch, *args, place_in=VMEM, place_out=VMEM, limit=LIMIT):
    return pl.pallas_call(
        kernel,
        out_shape=[jax.ShapeDtypeStruct(o, bf16) for o in outs],
        in_specs=[place_in] * len(args),
        out_specs=[place_out] * len(outs),
        scratch_shapes=scratch,
        compiler_params=pltpu.CompilerParams(vmem_limit_bytes=limit),
    )(*args)


def exchange(x, axes):
    return lax.all_to_all(x, axes, split_axis=0, concat_axis=0, tiled=True)


def per_device(queries, keys, values, grad_out, doc_lengths, positions):
    units, size = 256 * UNIT, UNIT * 32
    wide, narrow = (LOCAL, KVH * GROUP * HD), (LOCAL, KVH * HD)
    local = [pltpu.VMEM(s, bf16) for s in (wide, narrow, narrow, wide)]
    runs = jnp.pad(positions[::RUN] // RUN, (0, 4), constant_values=-1000)
    table = pl.pallas_call(
        table_kernel,
        out_shape=[
            jax.ShapeDtypeStruct(((BACK + 1) * BLOCK, BLOCK), bf16),
            jax.ShapeDtypeStruct((BLOCK, BLOCK), bf16),
            jax.ShapeDtypeStruct((size, size), bf16),
            jax.ShapeDtypeStruct((1, BLOCK), i32),
        ],
        in_specs=[VMEM, VMEM, pl.BlockSpec(memory_space=pltpu.SMEM)],
        out_specs=[VMEM] * 4,
        compiler_params=pltpu.CompilerParams(vmem_limit_bytes=LIMIT),
        cost_estimate=pl.CostEstimate(flops=1 << 24, bytes_accessed=1 << 18, transcendentals=0),
    )
    place_sort, place_unsort, place_unpack, begin = table(
        runs.reshape(1, 64), runs.reshape(64, 1), doc_lengths
    )
    (packed,) = call(
        pack_kernel,
        [(units, HD)],
        local
        + [
            pltpu.VMEM((size, KVH * HD), bf16),
            pltpu.VMEM((units, HD), bf16),
            pltpu.SemaphoreType.DMA((4,)),
            pltpu.SemaphoreType.DMA((4,)),
        ],
        queries,
        keys,
        values,
        grad_out,
        place_in=ANY,
        limit=None,
        place_out=ANY,
    )
    spread = exchange(packed.reshape(256, UNIT // 2, 2, HD), ALL).reshape(units, HD)
    (ordered,) = call(
        sort_kernel,
        [(BLOCK, 2048)],
        [pltpu.VMEM((units + 16, HD), f32)],
        spread,
        place_sort,
    )
    block = exchange(ordered.reshape(SPREAD, 8, 2048), SEQ_AXES).reshape(BLOCK, 2048)
    square = (GROUP * BLOCK, (BACK + 1) * BLOCK)
    (done,) = call(
        attention_kernel,
        [(BLOCK, 2048)],
        [
            pltpu.VMEM((square[1], BLOCK), f32),
            pltpu.VMEM(square, f32),
            pltpu.VMEM(square, f32),
            pltpu.VMEM(square, bf16),
            pltpu.VMEM(square, bf16),
        ]
        + [pltpu.VMEM((square[1], HD), f32)] * 2,
        begin,
        block,
    )
    back = exchange(done.reshape(SPREAD, 8, 2048), SEQ_AXES)
    (unsorted,) = call(
        unsort_kernel,
        [(units, HD)],
        [
            pltpu.VMEM((units + 16, HD), f32),
            pltpu.VMEM((BLOCK, 256), f32),
            pltpu.VMEM((BLOCK, 1280), bf16),
        ],
        back,
        place_unsort,
    )
    home = exchange(unsorted.reshape(256, UNIT // 2, 2, HD), ALL).reshape(units, HD)
    return tuple(
        call(
            unpack_kernel,
            [wide, wide, narrow, narrow],
            local + [pltpu.SemaphoreType.DMA((6,))],
            home,
            place_unpack,
            place_out=ANY,
        )
    )


def solution(mesh):
    parts = {"head": (("z_hi", 4), ("core", 2)), "inner": (("y", 4),), "outer": (("z_lo", 2), ("x", 4))}
    axes = [part for name in mesh.axis_names for part in parts[name]]
    split = Mesh(mesh.devices.reshape([size for _, size in axes]), [name for name, _ in axes])
    rows = P(ROWS, None)
    return jax.shard_map(
        per_device,
        mesh=split,
        in_specs=(rows, rows, rows, rows, P(), P()),
        out_specs=(rows, rows, rows, rows),
        check_vma=False,
    )
```
